32 devices in a mesh: grp: 4 (over x, core), blk: 8 (over z, y).
Axes of the slice: x: 2, y: 2, z: 4, core: 2. Of those that a mesh axis runs over, the one named last changes fastest.
Arguments:
- amplitudes: bfloat16 [64, 8, 256, 256], P('grp', None, 'blk'), may hold values from -6 to 6
- chol_vv: bfloat16 [4, 8, 256, 256], P('grp'), may hold values from -0.375 to 0.375
- chol_irrep: int32 [4], replicated, may hold values from 0 to 7
- pair_occ: int32 [64, 2], replicated, may hold values from 0 to 239
- occ_irrep: int32 [240], replicated, may hold values from 0 to 7
- vir_count: int32 [8], replicated, may hold values from 128 to 256, as said below
- ov_left: bfloat16 [4096, 8, 256], P(('grp', 'blk')), may hold values from -1.5 to 1.5
- ov_right: bfloat16 [4096, 8, 256], P(('grp', 'blk')), may hold values from -1.5 to 1.5
Outputs:
- residual: bfloat16 [64, 8, 256, 256], P('grp', None, 'blk')
The draws below stay inside these ranges and needn't reach their ends.
Inputs may be any that keep to these rules, and one draw needn't show every extreme that they name: `vir_count`: one irrep block is full in every draw; slots of a block beyond its count are padding.
All inputs are finite; a program needn't handle non-finite values.
Results may differ from the reference program's by a relative error of at most 0.0049.
Values may be sent and summed in bfloat16 or wider, within the bound.
No kernel may reach another device: no remote copies, remote signals or barrier semaphores. Data moves between devices by JAX's collectives and lax.ppermute only.
A program may use at most 192 MiB of HBM per device.

```python
import math
import jax
import jax.numpy as jnp
from jax import lax

IRREPS = 8
SLOTS = 256
OCC = 240
PAIRS = 64
CHOL = 4
OV_ROWS = 4096


def draw_vir_count(key, part):
    counts = jax.random.randint(key, (IRREPS,), SLOTS // 2, SLOTS + 1)
    full_block = jax.random.randint(jax.random.fold_in(key, 7), (), 0, IRREPS)
    return jnp.where(jnp.arange(IRREPS) == full_block, SLOTS, counts).astype(jnp.int32)


def with_ends(entries, rng, smallest, largest):
    spot = [jax.random.randint(jax.random.fold_in(rng, axis), (), 0, length) for axis, length in enumerate(entries.shape)]
    longest = entries.shape.index(max(entries.shape))
    neighbour = spot[:longest] + [(spot[longest] + 1) % entries.shape[longest]] + spot[longest + 1:]
    return entries.at[tuple(spot)].set(smallest).at[tuple(neighbour)].set(largest)


def shard_levels(rng, extent, pieces, low, top_value):
    loudness, own = 1.0, jax.random.fold_in(rng, 6)
    for axis_at, parts in pieces:
        heights = jnp.exp(jax.random.uniform(jax.random.fold_in(own, axis_at), (parts,), jnp.float32, low / len(pieces), top_value / len(pieces)))
        loudness = loudness * jnp.repeat(heights, extent[axis_at] // parts).reshape([-1 if axis == axis_at else 1 for axis in range(len(extent))])
    return loudness


def normal_values(key, dims, width, reach, cuts=(), kind=jnp.bfloat16):
    values = jax.random.normal(key, dims, jnp.float32) * width
    if len(cuts) > 0:
        values = shard_levels(key, dims, cuts, -0.22, 0.18) * values
    return jnp.clip(values, min=-reach, max=reach).astype(kind)


def setup_inputs(seed: int = 0) -> dict:
    key_of = jax.random.split(jax.random.key(seed), 9)
    amplitudes = normal_values(key_of[0], (PAIRS, IRREPS, SLOTS, SLOTS), 1.0, 6.0, ((0, 4), (2, 8)))
    chol_vv = normal_values(key_of[1], (CHOL, IRREPS, SLOTS, SLOTS), SLOTS ** -0.5, 0.375, ((0, 4),))
    chol_irrep = with_ends(jax.random.randint(key_of[2], (CHOL,), 0, 8), jax.random.fold_in(key_of[2], 1), 0, 7).astype(jnp.int32)
    pair_occ = with_ends(jax.random.randint(key_of[3], (PAIRS, 2), 0, OCC), jax.random.fold_in(key_of[3], 1), 0, OCC - 1).astype(jnp.int32)
    occ_irrep = with_ends(jax.random.randint(key_of[4], (OCC,), 0, 8), jax.random.fold_in(key_of[4], 1), 0, 7).astype(jnp.int32)
    vir_count = draw_vir_count(jax.random.fold_in(key_of[8], 71), 0)
    ov_left = normal_values(key_of[6], (OV_ROWS, IRREPS, SLOTS), 0.25, 1.5, ((0, 32),))
    ov_right = normal_values(key_of[7], (OV_ROWS, IRREPS, SLOTS), 0.25, 1.5, ((0, 32),))
    return {"amplitudes": amplitudes, "chol_vv": chol_vv, "chol_irrep": chol_irrep, "pair_occ": pair_occ, "occ_irrep": occ_irrep, "vir_count": vir_count, "ov_left": ov_left, "ov_right": ov_right}


def reference(amplitudes, chol_vv, chol_irrep, pair_occ, occ_irrep, vir_count, ov_left, ov_right):
    irrep_ids = jnp.arange(IRREPS, dtype=jnp.int32)
    slot_ids = jnp.arange(SLOTS, dtype=jnp.int32)
    slot_mask = (slot_ids[None, :] < vir_count[:, None]).astype(jnp.float32)
    pair_irrep = jnp.bitwise_xor(occ_irrep[pair_occ[:, 0]], occ_irrep[pair_occ[:, 1]]).astype(jnp.int32)
    vec_cols = jnp.bitwise_xor(irrep_ids[None, :], chol_irrep[:, None]).astype(jnp.int32)
    left_all = chol_vv * (slot_mask[None, :, :, None] * slot_mask[vec_cols][:, :, None, :]).astype(jnp.bfloat16)
    coupling = jnp.einsum('rhs,rht->hst', ov_left.astype(jnp.float32), ov_right.astype(jnp.float32))
    coupling = coupling * (1.0 / math.sqrt(OV_ROWS))
    coupling_bf = coupling.astype(jnp.bfloat16)

    def one_pair(inputs):
        pair_tile, pair_sym = inputs
        col_index = jnp.bitwise_xor(irrep_ids, pair_sym).astype(jnp.int32)
        col_mask = slot_mask[col_index]
        masked = pair_tile * (slot_mask[:, :, None] * col_mask[:, None, :]).astype(jnp.bfloat16)

        def add_vector(q, running):
            left_tile = left_all[q]
            block_perm = jnp.bitwise_xor(irrep_ids, chol_irrep[q]).astype(jnp.int32)
            shifted = masked[block_perm]
            half_product = jnp.einsum('hac,hcd->had', left_tile.astype(jnp.float32), shifted.astype(jnp.float32)).astype(jnp.bfloat16)
            right_tile = left_tile[col_index]
            return running + jnp.einsum('had,hbd->hab', half_product.astype(jnp.float32), right_tile.astype(jnp.float32))
        ladder = lax.fori_loop(0, CHOL, add_vector, jnp.zeros((IRREPS, SLOTS, SLOTS), jnp.float32))
        dress_one = jnp.einsum('hac,hcb->hab', masked.astype(jnp.float32), coupling_bf[col_index].astype(jnp.float32))
        dress_two = jnp.einsum('hac,hcb->hab', coupling_bf.astype(jnp.float32), masked.astype(jnp.float32))
        out_mask = slot_mask[:, :, None] * col_mask[:, None, :]
        return (out_mask * (ladder + dress_one + dress_two)).astype(jnp.bfloat16)
    return lax.map(one_pair, (amplitudes, pair_irrep))
```

```python
import functools
import math

import jax
import jax.numpy as jnp
from jax import lax
from jax.experimental import pallas as pl
from jax.experimental.pallas import tpu as pltpu
from jax.sharding import PartitionSpec as P

IRREPS = 8


def xor_permute(value, axis, count, bits):
    return lax.ppermute(value, axis, [(i, i ^ bits) for i in range(count)])


def pair_kernel(
    blk_count, slab_count, scalars, *refs
):
    piece_refs = refs[:blk_count]
    slab_refs = refs[blk_count : blk_count + slab_count]
    coupling_ref = refs[blk_count + slab_count]
    out_refs = refs[blk_count + slab_count + 1 : 2 * blk_count + slab_count + 1]
    assembled, masked, total = refs[2 * blk_count + slab_count + 1 :]
    rows = piece_refs[0].shape[1]
    slots = piece_refs[0].shape[2]
    sym = scalars[IRREPS]
    me = scalars[IRREPS + 1]

    def assemble(h, carry):
        for s in range(blk_count):
            start = pl.multiple_of((me ^ s) * rows, rows)
            assembled[pl.ds(start, rows), :] = piece_refs[s][h].astype(jnp.float32)
        row_ids = lax.broadcasted_iota(jnp.int32, (slots, slots), 0)
        col_ids = lax.broadcasted_iota(jnp.int32, (slots, slots), 1)
        keep = (row_ids < scalars[h]) & (col_ids < scalars[h ^ sym])
        masked[h] = jnp.where(keep, assembled[...], 0.0).astype(jnp.bfloat16)
        return carry

    lax.fori_loop(0, IRREPS, assemble, 0)

    def one_block(h, carry):
        col = h ^ sym
        acc = jnp.dot(masked[h], coupling_ref[col], preferred_element_type=jnp.float32)
        acc += jnp.dot(coupling_ref[h], masked[h], preferred_element_type=jnp.float32)
        for q in range(slab_count):
            half = jnp.dot(
                slab_refs[q][h], masked[h ^ scalars[IRREPS + 2 + q]], preferred_element_type=jnp.float32
            ).astype(jnp.bfloat16)
            acc += lax.dot_general(
                half, slab_refs[q][col], (((1,), (1,)), ((), ())), preferred_element_type=jnp.float32
            )
        row_ids = lax.broadcasted_iota(jnp.int32, (slots, slots), 0)
        col_ids = lax.broadcasted_iota(jnp.int32, (slots, slots), 1)
        keep = (row_ids < scalars[h]) & (col_ids < scalars[col])
        total[...] = jnp.where(keep, acc, 0.0)
        for s in range(blk_count):
            start = pl.multiple_of((me ^ s) * rows, rows)
            out_refs[s][h] = total[pl.ds(start, rows), :].astype(jnp.bfloat16)
        return carry

    lax.fori_loop(0, IRREPS, one_block, 0)


def pair_call(scalars, pieces, slabs, coupling):
    blk_count, slab_count = len(pieces), len(slabs)
    rows, slots = pieces[0].shape[1:]
    vmem = pl.BlockSpec(memory_space=pltpu.VMEM)
    flops = IRREPS * (2 * slab_count + 2) * 2 * slots**3
    return pl.pallas_call(
        functools.partial(pair_kernel, blk_count, slab_count),
        out_shape=[jax.ShapeDtypeStruct((IRREPS, rows, slots), jnp.bfloat16)] * blk_count,
        in_specs=[pl.BlockSpec(memory_space=pltpu.SMEM)] + [vmem] * (blk_count + slab_count + 1),
        out_specs=[vmem] * blk_count,
        scratch_shapes=[
            pltpu.VMEM((slots, slots), jnp.float32),
            pltpu.VMEM((IRREPS, slots, slots), jnp.bfloat16),
            pltpu.VMEM((slots, slots), jnp.float32),
        ],
        compiler_params=pltpu.CompilerParams(vmem_limit_bytes=40 * 1024 * 1024),
        cost_estimate=pl.CostEstimate(flops=flops, bytes_accessed=16 * slots**2 * 10, transcendentals=0),
    )(scalars, *pieces, *slabs, coupling)


def coupling_blocks(ov_left, ov_right, grp_count, blk_count):
    rows, _, slots = ov_left.shape
    per_grp = IRREPS // grp_count
    grp, blk = lax.axis_index("grp"), lax.axis_index("blk")
    factors = jnp.stack([ov_left, ov_right]).transpose(2, 0, 1, 3)
    parts = [
        lax.dynamic_slice_in_dim(factors, (grp ^ s) * per_grp, per_grp, 0) for s in range(grp_count)
    ]
    parts = [parts[0]] + [xor_permute(parts[s], "grp", grp_count, s) for s in range(1, grp_count)]
    gathered = jnp.concatenate(parts, axis=2)
    local = jnp.einsum(
        "hrs,hrt->hst", gathered[:, 0], gathered[:, 1], preferred_element_type=jnp.float32
    )
    scale = 1.0 / math.sqrt(rows * grp_count * blk_count)
    flat = local.reshape(per_grp * slots, slots)
    half_rows = per_grp * slots // 2
    low, high = blk % 2, blk // 2
    away = lax.dynamic_slice_in_dim(flat, (1 - low) * half_rows, half_rows, 0)
    kept = lax.dynamic_slice_in_dim(flat, low * half_rows, half_rows, 0)
    kept = kept + xor_permute(away, "blk", blk_count, 1)
    highs = blk_count // 2
    piece = half_rows // highs
    own = lax.dynamic_slice_in_dim(kept, high * piece, piece, 0)
    for s in range(1, highs):
        away = lax.dynamic_slice_in_dim(kept, (high ^ s) * piece, piece, 0)
        own = own + xor_permute(away, "blk", blk_count, 2 * s)
    own = (own * scale).astype(jnp.bfloat16)
    half = jnp.zeros((half_rows, slots), jnp.bfloat16)
    half = lax.dynamic_update_slice_in_dim(half, own, high * piece, 0)
    for s in range(1, highs):
        came = xor_permute(own, "blk", blk_count, 2 * s)
        half = lax.dynamic_update_slice_in_dim(half, came, (high ^ s) * piece, 0)
    same_core = jnp.zeros((grp_count // 2, 2, half_rows, slots), jnp.bfloat16)
    for dx in range(grp_count // 2):
        for dy in range(2):
            came = half
            if dx or dy:
                flat_ids = [(g, b) for g in range(grp_count) for b in range(blk_count)]
                perm = [
                    (g * blk_count + b, (g ^ (2 * dx)) * blk_count + (b ^ dy)) for g, b in flat_ids
                ]
                came = lax.ppermute(half, ("grp", "blk"), perm)
            same_core = lax.dynamic_update_slice(
                same_core, came[None, None], ((grp // 2) ^ dx, low ^ dy, 0, 0)
            )
    other_core = xor_permute(same_core, "grp", grp_count, 1)
    core = grp % 2
    first = jnp.where(core == 0, same_core, other_core)
    second = jnp.where(core == 0, other_core, same_core)
    return jnp.stack([first, second], axis=1).reshape(IRREPS, slots, slots), gathered


def per_device(amplitudes, chol_vv, chol_irrep, pair_occ, occ_irrep, vir_count, ov_left, ov_right):
    blk_count = lax.axis_size("blk")
    grp_count = lax.axis_size("grp")
    pair_total, _, rows, slots = amplitudes.shape
    per_dev = pair_total // blk_count
    grp, blk = lax.axis_index("grp"), lax.axis_index("blk")

    pieces = [None] * blk_count
    for s in reversed(range(blk_count)):
        block = lax.dynamic_slice_in_dim(amplitudes, (blk ^ s) * per_dev, per_dev, 0)
        pieces[s] = xor_permute(block, "blk", blk_count, s) if s else block

    coupling, after = coupling_blocks(ov_left, ov_right, grp_count, blk_count)

    per_slab = chol_vv.shape[0]
    chol_vv, _ = lax.optimization_barrier((chol_vv, after))
    same = [chol_vv] + [
        xor_permute(chol_vv, "grp", grp_count, 2 * s) for s in range(1, grp_count // 2)
    ]
    other = [xor_permute(slab, "grp", grp_count, 1) for slab in same]
    slabs, owners = [], []
    for s in range(grp_count // 2):
        for c, group in enumerate((same, other)):
            for k in range(per_slab):
                slabs.append(group[s][k])
                owners.append((grp ^ (2 * s + c)) * per_slab + k)
    slab_irreps = chol_irrep[jnp.stack(owners)]

    pair_start = (grp * blk_count + blk) * per_dev
    own_pairs = lax.dynamic_slice_in_dim(pair_occ, pair_start, per_dev, 0)
    occ_ids = jnp.arange(occ_irrep.shape[0], dtype=jnp.int32)
    one_hot = own_pairs[:, :, None] == occ_ids[None, None, :]
    labels = jnp.sum(jnp.where(one_hot, occ_irrep[None, None, :], 0), axis=2)
    pair_irrep = jnp.bitwise_xor(labels[:, 0], labels[:, 1])

    result = jnp.zeros(amplitudes.shape, jnp.bfloat16)
    for j in range(per_dev):
        scalars = jnp.concatenate(
            [vir_count, pair_irrep[j : j + 1], blk[None].astype(jnp.int32), slab_irreps]
        )
        outs = pair_call(scalars, [piece[j] for piece in pieces], slabs, coupling)
        for s in reversed(range(blk_count)):
            came = xor_permute(outs[s], "blk", blk_count, s) if s else outs[s]
            result = lax.dynamic_update_slice(
                result, came[None], ((blk ^ s) * per_dev + j, 0, 0, 0)
            )
    return result


def solution(mesh):
    return jax.shard_map(
        per_device,
        mesh=mesh,
        in_specs=(
            P("grp", None, "blk", None),
            P("grp", None, None, None),
            P(),
            P(),
            P(),
            P(),
            P(("grp", "blk"), None, None),
            P(("grp", "blk"), None, None),
        ),
        out_specs=P("grp", None, "blk", None),
        check_vma=False,
    )
```

```python
import functools
import math

import jax
import jax.numpy as jnp
from jax import lax
from jax.experimental import pallas as pl
from jax.experimental.pallas import tpu as pltpu
from jax.sharding import PartitionSpec as P

IRREPS = 8


def xor_permute(value, axis, count, bits):
    return lax.ppermute(value, axis, [(i, i ^ bits) for i in range(count)])


def ladder_kernel(which, slab_at, part_counts, scalars, piece_ref, *refs):
    part_refs, (ladder_ref, masked_ref, assembled, joined) = refs[:-4], refs[-4:]
    slab_refs, at, room = [], 0, 0
    for parts in part_counts:
        if parts == 1:
            slab_refs.append(part_refs[at])
        else:
            size = IRREPS // parts
            for k in range(parts):
                joined[room, k * size : (k + 1) * size] = part_refs[at + k][...]
            slab_refs.append(joined.at[room])
            room += 1
        at += parts
    blk_count, _, _, rows, slots = piece_ref.shape
    sym = scalars[IRREPS + which]
    whole_tiles = rows % 16 == 0
    row_ids = lax.broadcasted_iota(jnp.int32, (rows, slots), 0)
    col_ids = lax.broadcasted_iota(jnp.int32, (rows, slots), 1)

    def mask(h, carry):
        in_cols = col_ids < scalars[h ^ sym]
        for owner in range(blk_count):
            keep = in_cols & (row_ids < scalars[h] - owner * rows)
            block = jnp.where(keep, piece_ref[owner, which, h].astype(jnp.float32), 0.0)
            at = slice(owner * rows, (owner + 1) * rows)
            if whole_tiles:
                masked_ref[h, at, :] = block.astype(jnp.bfloat16)
            else:
                assembled[at, :] = block
        if not whole_tiles:
            masked_ref[h] = assembled[...].astype(jnp.bfloat16)
        return carry

    lax.fori_loop(0, IRREPS, mask, 0, unroll=2)

    def one_block(h, carry):
        acc = None
        for q, slab in enumerate(slab_refs):
            shift = scalars[slab_at + q]
            half = jnp.dot(
                slab[h], masked_ref[h ^ shift], preferred_element_type=jnp.float32
            ).astype(jnp.bfloat16)
            term = lax.dot_general(
                half, slab[h ^ sym], (((1,), (1,)), ((), ())), preferred_element_type=jnp.float32
            )
            acc = term if acc is None else acc + term
        ladder_ref[h] = acc
        return carry

    lax.fori_loop(0, IRREPS, one_block, 0, unroll=max(1, 32 // len(slab_refs)))


def ladder_call(scalars, which, slab_at, pieces, slabs):
    slots = pieces.shape[-1]
    vmem = pl.BlockSpec(memory_space=pltpu.VMEM)
    flops = IRREPS * 2 * len(slabs) * 2 * slots**3
    parts = [part for slab in slabs for part in slab]
    part_counts = [len(slab) for slab in slabs]
    rooms = max(1, sum(count > 1 for count in part_counts))
    return pl.pallas_call(
        functools.partial(ladder_kernel, which, slab_at, part_counts),
        out_shape=[
            jax.ShapeDtypeStruct((IRREPS, slots, slots), jnp.float32),
            jax.ShapeDtypeStruct((IRREPS, slots, slots), jnp.bfloat16),
        ],
        in_specs=[pl.BlockSpec(memory_space=pltpu.SMEM)] + [vmem] * (1 + len(parts)),
        out_specs=[vmem] * 2,
        scratch_shapes=[
            pltpu.VMEM((slots, slots), jnp.float32),
            pltpu.VMEM((rooms, IRREPS, slots, slots), jnp.bfloat16),
        ],
        compiler_params=pltpu.CompilerParams(vmem_limit_bytes=20 * 1024 * 1024),
        cost_estimate=pl.CostEstimate(
            flops=flops, bytes_accessed=10 * 1024 * 1024, transcendentals=0
        ),
    )(scalars, pieces, *parts)


def dress_kernel(per_dev, core_at, scalars, same_ref, other_ref, *refs):
    ladder_refs, masked_refs = refs[: 2 * per_dev : 2], refs[1 : 2 * per_dev : 2]
    out_ref, coupling = refs[2 * per_dev :]
    blk_count, _, _, rows, slots = out_ref.shape
    core = scalars[core_at]
    half = same_ref.shape[0]
    for k in range(half):
        coupling[core * half + k] = same_ref[k]
        coupling[(1 - core) * half + k] = other_ref[k]
    row_ids = lax.broadcasted_iota(jnp.int32, (slots, slots), 0)
    col_ids = lax.broadcasted_iota(jnp.int32, (slots, slots), 1)

    def one_block(h, carry):
        for j in range(per_dev):
            col = h ^ scalars[IRREPS + j]
            block = masked_refs[j][h]
            acc = ladder_refs[j][h]
            acc += jnp.dot(block, coupling[col], preferred_element_type=jnp.float32)
            acc += jnp.dot(coupling[h], block, preferred_element_type=jnp.float32)
            keep = (row_ids < scalars[h]) & (col_ids < scalars[col])
            acc = jnp.where(keep, acc, 0.0)
            for owner in range(blk_count):
                part = acc[owner * rows : (owner + 1) * rows, :]
                out_ref[owner, j, h] = part.astype(jnp.bfloat16)
        return carry

    lax.fori_loop(0, IRREPS, one_block, 0, unroll=2)


def dress_call(scalars, core_at, blk_count, ladders, same_core, other_core):
    per_dev, slots = len(ladders), same_core.shape[-1]
    vmem = pl.BlockSpec(memory_space=pltpu.VMEM)
    return pl.pallas_call(
        functools.partial(dress_kernel, per_dev, core_at),
        out_shape=jax.ShapeDtypeStruct(
            (blk_count, per_dev, IRREPS, slots // blk_count, slots), jnp.bfloat16
        ),
        in_specs=[pl.BlockSpec(memory_space=pltpu.SMEM)] + [vmem] * (2 + 2 * per_dev),
        out_specs=vmem,
        scratch_shapes=[pltpu.VMEM((IRREPS, slots, slots), jnp.bfloat16)],
        compiler_params=pltpu.CompilerParams(vmem_limit_bytes=20 * 1024 * 1024),
        cost_estimate=pl.CostEstimate(
            flops=per_dev * IRREPS * 4 * slots**3, bytes_accessed=8 * 1024 * 1024, transcendentals=0
        ),
    )(scalars, same_core, other_core, *[one for pair in ladders for one in pair])


def after(value, *others):
    return lax.optimization_barrier((value, *others))[0]


def factor_kernel(kept, came, out_ref):
    dims = (((0,), (0,)), ((), ()))
    for h in range(out_ref.shape[0]):
        total = lax.dot_general(kept[h, 0], kept[h, 1], dims, preferred_element_type=jnp.float32)
        total += lax.dot_general(came[h, 0], came[h, 1], dims, preferred_element_type=jnp.float32)
        out_ref[h] = total.astype(out_ref.dtype)


def plane_permute(value, grp_count, blk_count, dx, dy):
    perm = [
        (g * blk_count + b, (g ^ (2 * dx)) * blk_count + (b ^ dy))
        for g in range(grp_count)
        for b in range(blk_count)
    ]
    return lax.ppermute(value, ("grp", "blk"), perm)


def per_device(amplitudes, chol_vv, chol_irrep, pair_occ, occ_irrep, vir_count, ov_left, ov_right):
    blk_count = lax.axis_size("blk")
    grp_count = lax.axis_size("grp")
    pair_total, _, rows, slots = amplitudes.shape
    per_dev = pair_total // blk_count
    grp, blk = lax.axis_index("grp"), lax.axis_index("blk")

    by_dest = amplitudes.reshape(blk_count, per_dev, IRREPS, rows, slots)
    all_rows = lax.all_to_all(by_dest, "blk", split_axis=0, concat_axis=0, tiled=True)

    ov_rows = ov_left.shape[0]
    low_count = IRREPS // grp_count
    core, x, low = grp % 2, grp // 2, blk % low_count
    planes = [(dx, dy) for dx in range(grp_count // 2) for dy in range(low_count)]
    half = len(planes)
    factors = jnp.stack([ov_left, ov_right]).transpose(2, 0, 1, 3)
    kept = lax.dynamic_slice_in_dim(factors, core * half, half, 0)
    away = lax.dynamic_slice_in_dim(factors, (1 - core) * half, half, 0)
    came = xor_permute(away, "grp", grp_count, 1)
    vmem = pl.BlockSpec(memory_space=pltpu.VMEM)
    local = pl.pallas_call(
        factor_kernel,
        out_shape=jax.ShapeDtypeStruct((half, slots, slots), jnp.bfloat16),
        in_specs=[vmem] * 2,
        out_specs=vmem,
    )(kept, came)
    per_slab = chol_vv.shape[0]
    cut = IRREPS // 2

    def along_x(part):
        return [xor_permute(part, "grp", grp_count, 2 * s) for s in range(1, grp_count // 2)]

    def other_core_of(parts):
        return [xor_permute(part, "grp", grp_count, 1) for part in parts]

    first_half = along_x(chol_vv[:, :cut])

    parts = []
    for dx, dy in planes:
        at = (x ^ dx) * low_count + (low ^ dy)
        part = lax.dynamic_index_in_dim(local, at, 0, keepdims=False)
        if dx or dy:
            part = plane_permute(part, grp_count, blk_count, dx, dy)
        parts.append(part.astype(jnp.float32))
    total = sum(parts).astype(jnp.bfloat16)
    total = after(total, *first_half)
    second_half = along_x(after(chol_vv[:, cut:], total))
    same = [(chol_vv,)] + list(zip(first_half, second_half))
    own_other = other_core_of([chol_vv])
    other = [(own_other[0],)] + list(zip(other_core_of(first_half), other_core_of(second_half)))

    bit = low_count
    while bit < blk_count:
        came = xor_permute(total, "blk", blk_count, bit)
        summed = total.astype(jnp.float32) + came.astype(jnp.float32)
        bit *= 2
        total = summed.astype(jnp.bfloat16)
    scale = 1.0 / math.sqrt(ov_rows * grp_count * blk_count)
    block = (summed * scale).astype(jnp.bfloat16)
    slabs, owners = [], []
    for s in range(grp_count // 2):
        for c, group in enumerate((same, other)):
            for k in range(per_slab):
                slabs.append([part[k] for part in group[s]])
                owners.append((grp ^ (2 * s + c)) * per_slab + k)
    slab_irreps = chol_irrep[jnp.stack(owners)]

    pair_start = (grp * blk_count + blk) * per_dev
    own_pairs = lax.dynamic_slice_in_dim(pair_occ, pair_start, per_dev, 0)
    occ_ids = jnp.arange(occ_irrep.shape[0], dtype=jnp.int32)
    one_hot = own_pairs[:, :, None] == occ_ids[None, None, :]
    labels = jnp.sum(jnp.where(one_hot, occ_irrep[None, None, :], 0), axis=2)
    pair_irrep = jnp.bitwise_xor(labels[:, 0], labels[:, 1])

    scalars = jnp.concatenate([vir_count, pair_irrep, slab_irreps, core[None].astype(jnp.int32)])
    slab_at = IRREPS + per_dev
    ladders = [ladder_call(scalars, j, slab_at, all_rows, slabs) for j in range(per_dev)]

    got = [
        plane_permute(block, grp_count, blk_count, dx, dy) if dx or dy else block
        for dx, dy in planes
    ]
    got, ladders[0] = lax.optimization_barrier((tuple(got), ladders[0]))
    same_core = jnp.zeros((half, slots, slots), jnp.bfloat16)
    for (dx, dy), one in zip(planes, got):
        at = (x ^ dx) * low_count + (low ^ dy)
        same_core = lax.dynamic_update_slice(same_core, one[None], (at, 0, 0))
    other_core = xor_permute(same_core, "grp", grp_count, 1)
    if per_dev > 1:
        other_core, ladders[1:] = lax.optimization_barrier((other_core, ladders[1:]))
    core_at = slab_at + len(slabs)
    sent = dress_call(scalars, core_at, blk_count, ladders, same_core, other_core)
    result = lax.all_to_all(sent, "blk", split_axis=0, concat_axis=0, tiled=True)
    return result.reshape(amplitudes.shape)


def solution(mesh):
    return jax.shard_map(
        per_device,
        mesh=mesh,
        in_specs=(
            P("grp", None, "blk", None),
            P("grp", None, None, None),
            P(),
            P(),
            P(),
            P(),
            P(("grp", "blk"), None, None),
            P(("grp", "blk"), None, None),
        ),
        out_specs=P("grp", None, "blk", None),
        check_vma=False,
    )
```

```python
import functools
import math

import jax
import jax.numpy as jnp
from jax import lax
from jax.experimental import pallas as pl
from jax.experimental.pallas import tpu as pltpu
from jax.sharding import PartitionSpec as P

IRREPS = 8


def xor_permute(value, axis, count, bits):
    return lax.ppermute(value, axis, [(i, i ^ bits) for i in range(count)])


def ladder_kernel(which, slab_at, part_counts, scalars, piece_ref, *refs):
    part_refs, (ladder_ref, masked_ref, assembled, joined) = refs[:-4], refs[-4:]
    slab_refs, at, room = [], 0, 0
    for parts in part_counts:
        if parts == 1:
            slab_refs.append(part_refs[at])
        else:
            begin = 0
            for part in part_refs[at : at + parts]:
                joined[room, begin : begin + part.shape[0]] = part[...]
                begin += part.shape[0]
            slab_refs.append(joined.at[room])
            room += 1
        at += parts
    blk_count, _, _, rows, slots = piece_ref.shape
    sym = scalars[IRREPS + which]
    whole_tiles = rows % 16 == 0
    row_ids = lax.broadcasted_iota(jnp.int32, (rows, slots), 0)
    col_ids = lax.broadcasted_iota(jnp.int32, (rows, slots), 1)

    def mask(h, carry):
        ones = jnp.where(col_ids < scalars[h ^ sym], 1.0, 0.0)
        for owner in range(blk_count):
            in_rows = row_ids < scalars[h] - owner * rows
            keep = jnp.where(in_rows, ones, 0.0).astype(jnp.bfloat16)
            block = piece_ref[owner, which, h] * keep
            at = slice(owner * rows, (owner + 1) * rows)
            if whole_tiles:
                masked_ref[h, at, :] = block
            else:
                assembled[at, :] = block.astype(jnp.float32)
        if not whole_tiles:
            masked_ref[h] = assembled[...].astype(jnp.bfloat16)
        return carry

    lax.fori_loop(0, IRREPS, mask, 0, unroll=2)

    def one_block(h, carry):
        acc = None
        for q, slab in enumerate(slab_refs):
            shift = scalars[slab_at + q]
            half = jnp.dot(
                slab[h], masked_ref[h ^ shift], preferred_element_type=jnp.float32
            ).astype(jnp.bfloat16)
            term = lax.dot_general(
                half, slab[h ^ sym], (((1,), (1,)), ((), ())), preferred_element_type=jnp.float32
            )
            acc = term if acc is None else acc + term
        ladder_ref[h] = acc
        return carry

    lax.fori_loop(0, IRREPS, one_block, 0, unroll=max(1, 32 // len(slab_refs)))


def ladder_call(scalars, which, slab_at, pieces, slabs):
    slots = pieces.shape[-1]
    vmem = pl.BlockSpec(memory_space=pltpu.VMEM)
    flops = IRREPS * 2 * len(slabs) * 2 * slots**3
    parts = [part for slab in slabs for part in slab]
    part_counts = [len(slab) for slab in slabs]
    rooms = max(1, sum(count > 1 for count in part_counts))
    return pl.pallas_call(
        functools.partial(ladder_kernel, which, slab_at, part_counts),
        out_shape=[
            jax.ShapeDtypeStruct((IRREPS, slots, slots), jnp.float32),
            jax.ShapeDtypeStruct((IRREPS, slots, slots), jnp.bfloat16),
        ],
        in_specs=[pl.BlockSpec(memory_space=pltpu.SMEM)] + [vmem] * (1 + len(parts)),
        out_specs=[vmem] * 2,
        scratch_shapes=[
            pltpu.VMEM((slots, slots), jnp.float32),
            pltpu.VMEM((rooms, IRREPS, slots, slots), jnp.bfloat16),
        ],
        compiler_params=pltpu.CompilerParams(vmem_limit_bytes=16 * 1024 * 1024),
        cost_estimate=pl.CostEstimate(
            flops=flops, bytes_accessed=10 * 1024 * 1024, transcendentals=0
        ),
    )(scalars, pieces, *parts)


def dress_kernel(per_dev, planes, scalars, same_ref, other_ref, *refs):
    ladder_refs, masked_refs = refs[: 2 * per_dev : 2], refs[1 : 2 * per_dev : 2]
    out_refs, (coupling, total) = refs[2 * per_dev : -2], refs[-2:]
    blk_count = len(out_refs)
    _, _, rows, slots = out_refs[0].shape
    blk = lax.axis_index("blk")
    core = lax.axis_index("grp") % 2
    half = len(planes)
    for k, place in enumerate(plane_places(planes, IRREPS // lax.axis_size("grp"))):
        coupling[core * half + place] = same_ref[k]
        coupling[(1 - core) * half + place] = other_ref[k]
    row_ids = lax.broadcasted_iota(jnp.int32, (slots, slots), 0)
    col_ids = lax.broadcasted_iota(jnp.int32, (slots, slots), 1)

    def one_block(h, carry):
        for j in range(per_dev):
            col = h ^ scalars[IRREPS + j]
            block = masked_refs[j][h]
            acc = ladder_refs[j][h]
            acc += jnp.dot(block, coupling[col], preferred_element_type=jnp.float32)
            acc += jnp.dot(coupling[h], block, preferred_element_type=jnp.float32)
            keep = (row_ids < scalars[h]) & (col_ids < scalars[col])
            total[j] = jnp.where(keep, acc, 0.0)
            for s, out_ref in enumerate(out_refs):
                at = pl.ds(pl.multiple_of((blk ^ s) * rows, rows), rows)
                out_ref[j, h] = total[j, at, :].astype(jnp.bfloat16)
        return carry

    lax.fori_loop(0, IRREPS, one_block, 0, unroll=2)


def dress_call(scalars, planes, blk_count, ladders, same_core, other_core):
    per_dev, slots = len(ladders), same_core.shape[-1]
    vmem = pl.BlockSpec(memory_space=pltpu.VMEM)
    return pl.pallas_call(
        functools.partial(dress_kernel, per_dev, planes),
        out_shape=[
            jax.ShapeDtypeStruct((per_dev, IRREPS, slots // blk_count, slots), jnp.bfloat16)
        ]
        * blk_count,
        in_specs=[pl.BlockSpec(memory_space=pltpu.SMEM)] + [vmem] * (2 + 2 * per_dev),
        out_specs=[vmem] * blk_count,
        scratch_shapes=[
            pltpu.VMEM((IRREPS, slots, slots), jnp.bfloat16),
            pltpu.VMEM((per_dev, slots, slots), jnp.float32),
        ],
        compiler_params=pltpu.CompilerParams(vmem_limit_bytes=16 * 1024 * 1024),
        cost_estimate=pl.CostEstimate(
            flops=per_dev * IRREPS * 4 * slots**3, bytes_accessed=8 * 1024 * 1024, transcendentals=0
        ),
    )(scalars, same_core, other_core, *[one for pair in ladders for one in pair])


def after(value, *others):
    return lax.optimization_barrier((value, *others))[0]


def plane_places(planes, low_count):
    x, low = lax.axis_index("grp") // 2, lax.axis_index("blk") % low_count
    return [(x ^ dx) * low_count + (low ^ dy) for dx, dy in planes]


def factor_kernel(planes, low_count, kept, came, *out_refs):
    dims = (((0,), (0,)), ((), ()))
    for h, out_ref in zip(plane_places(planes, low_count), out_refs):
        total = lax.dot_general(kept[h, 0], kept[h, 1], dims, preferred_element_type=jnp.float32)
        total += lax.dot_general(came[h, 0], came[h, 1], dims, preferred_element_type=jnp.float32)
        out_ref[...] = total.astype(out_ref.dtype)


def plane_permute(value, grp_count, blk_count, dx, dy):
    perm = [
        (g * blk_count + b, (g ^ (2 * dx)) * blk_count + (b ^ dy))
        for g in range(grp_count)
        for b in range(blk_count)
    ]
    return lax.ppermute(value, ("grp", "blk"), perm)


def per_device(amplitudes, chol_vv, chol_irrep, pair_occ, occ_irrep, vir_count, ov_left, ov_right):
    blk_count = lax.axis_size("blk")
    grp_count = lax.axis_size("grp")
    pair_total, _, rows, slots = amplitudes.shape
    per_dev = pair_total // blk_count
    grp, blk = lax.axis_index("grp"), lax.axis_index("blk")

    by_dest = amplitudes.reshape(blk_count, per_dev, IRREPS, rows, slots)
    all_rows = lax.all_to_all(by_dest, "blk", split_axis=0, concat_axis=0, tiled=True)

    ov_rows = ov_left.shape[0]
    low_count = IRREPS // grp_count
    core, x, low = grp % 2, grp // 2, blk % low_count
    planes = [(dx, dy) for dx in range(grp_count // 2) for dy in range(low_count)]
    half = len(planes)
    factors = jnp.stack([ov_left, ov_right]).transpose(2, 0, 1, 3)
    kept = lax.dynamic_slice_in_dim(factors, core * half, half, 0)
    away = lax.dynamic_slice_in_dim(factors, (1 - core) * half, half, 0)
    came = xor_permute(away, "grp", grp_count, 1)
    vmem = pl.BlockSpec(memory_space=pltpu.VMEM)
    local = pl.pallas_call(
        functools.partial(factor_kernel, planes, low_count),
        out_shape=[jax.ShapeDtypeStruct((slots, slots), jnp.bfloat16)] * half,
        in_specs=[vmem] * 2,
        out_specs=[vmem] * half,
        compiler_params=pltpu.CompilerParams(vmem_limit_bytes=8 * 1024 * 1024),
    )(kept, came)
    per_slab = chol_vv.shape[0]
    cut = IRREPS // 2

    def along_x(part):
        return [xor_permute(part, "grp", grp_count, 2 * s) for s in range(1, grp_count // 2)]

    def other_core_of(parts):
        return [xor_permute(part, "grp", grp_count, 1) for part in parts]

    first_half = along_x(chol_vv[:, :cut])

    parts = []
    for (dx, dy), part in zip(planes, local):
        if dx or dy:
            part = plane_permute(part, grp_count, blk_count, dx, dy)
        parts.append(part.astype(jnp.float32))
    total = sum(parts)
    total = after(total, *first_half)
    second_half = along_x(after(chol_vv[:, cut:], total))
    same = [(chol_vv,)] + list(zip(first_half, second_half))
    own_other = other_core_of([chol_vv])
    other = [(own_other[0],)]
    for one, two in zip(first_half, second_half):
        mid = two.shape[1] // 2
        other.append(tuple(other_core_of([one, two[:, :mid], two[:, mid:]])))

    bit = low_count
    while bit < blk_count:
        came = xor_permute(total.astype(jnp.bfloat16), "blk", blk_count, bit)
        total = total + came.astype(jnp.float32)
        bit *= 2
    scale = 1.0 / math.sqrt(ov_rows * grp_count * blk_count)
    block = (total * scale).astype(jnp.bfloat16)
    slabs, owners = [], []
    for s in range(grp_count // 2):
        for c, group in enumerate((same, other)):
            for k in range(per_slab):
                slabs.append([part[k] for part in group[s]])
                owners.append((grp ^ (2 * s + c)) * per_slab + k)
    slab_irreps = chol_irrep[jnp.stack(owners)]

    pair_start = (grp * blk_count + blk) * per_dev
    own_pairs = lax.dynamic_slice_in_dim(pair_occ, pair_start, per_dev, 0)
    occ_ids = jnp.arange(occ_irrep.shape[0], dtype=jnp.int32)
    one_hot = own_pairs[:, :, None] == occ_ids[None, None, :]
    labels = jnp.sum(jnp.where(one_hot, occ_irrep[None, None, :], 0), axis=2)
    pair_irrep = jnp.bitwise_xor(labels[:, 0], labels[:, 1])

    scalars = jnp.concatenate([vir_count, pair_irrep, slab_irreps])
    slab_at = IRREPS + per_dev
    ladders = [ladder_call(scalars, j, slab_at, all_rows, slabs) for j in range(per_dev)]

    got = [
        plane_permute(block, grp_count, blk_count, dx, dy) if dx or dy else block
        for dx, dy in planes
    ]
    got, ladders[0] = lax.optimization_barrier((tuple(got), ladders[0]))
    same_core = jnp.stack(got)
    other_core = xor_permute(same_core, "grp", grp_count, 1)
    if per_dev > 1:
        other_core, ladders[1:] = lax.optimization_barrier((other_core, ladders[1:]))
    sent = dress_call(scalars, planes, blk_count, ladders, same_core, other_core)
    result = jnp.zeros(amplitudes.shape, jnp.bfloat16)
    result = lax.dynamic_update_slice(result, sent[0], (blk * per_dev, 0, 0, 0))
    top = blk_count // 2
    far, near = list(range(blk_count - 1, top - 1, -1)), list(range(top - 1, 0, -1))
    for s in [s for two in zip(far, near + [0]) for s in two if s]:
        came = xor_permute(sent[s], "blk", blk_count, s)
        result = lax.dynamic_update_slice(result, came, ((blk ^ s) * per_dev, 0, 0, 0))
    return result


def solution(mesh):
    return jax.shard_map(
        per_device,
        mesh=mesh,
        in_specs=(
            P("grp", None, "blk", None),
            P("grp", None, None, None),
            P(),
            P(),
            P(),
            P(),
            P(("grp", "blk"), None, None),
            P(("grp", "blk"), None, None),
        ),
        out_specs=P("grp", None, "blk", None),
        check_vma=False,
    )
```

```python
import functools
import math

import jax
import jax.numpy as jnp
from jax import lax
from jax.experimental import pallas as pl
from jax.experimental.pallas import tpu as pltpu
from jax.sharding import PartitionSpec as P

IRREPS = 8


def xor_permute(value, axis, count, bits):
    return lax.ppermute(value, axis, [(i, i ^ bits) for i in range(count)])


def join_parts(part_counts, part_refs, joined):
    slab_refs, at, room = [], 0, 0
    for parts in part_counts:
        if parts == 1:
            slab_refs.append(part_refs[at])
        else:
            begin = 0
            for part in part_refs[at : at + parts]:
                joined[room, begin : begin + part.shape[0]] = part[...]
                begin += part.shape[0]
            slab_refs.append(joined.at[room])
            room += 1
        at += parts
    return slab_refs


def add_slabs(scalars, slab_at, slab_refs, masked_ref, ladder_ref, before_ref):
    per_dev = masked_ref.shape[0]

    def one_block(h, carry):
        for j in range(per_dev):
            col = h ^ scalars[IRREPS + j]
            acc = None if before_ref is None else before_ref[j, h]
            for q, slab in enumerate(slab_refs):
                shift = scalars[slab_at + q]
                half = jnp.dot(
                    slab[h], masked_ref[j, h ^ shift], preferred_element_type=jnp.float32
                ).astype(jnp.bfloat16)
                term = lax.dot_general(
                    half, slab[col], (((1,), (1,)), ((), ())), preferred_element_type=jnp.float32
                )
                acc = term if acc is None else acc + term
            ladder_ref[j, h] = acc
        return carry

    lax.fori_loop(0, IRREPS, one_block, 0, unroll=max(1, 32 // (per_dev * len(slab_refs))))


def first_kernel(slab_at, part_counts, scalars, piece_ref, *refs):
    part_refs, (ladder_ref, masked_ref, assembled, joined) = refs[:-4], refs[-4:]
    blk_count, per_dev, _, rows, slots = piece_ref.shape
    whole_tiles = rows % 16 == 0
    row_ids = lax.broadcasted_iota(jnp.int32, (rows, slots), 0)
    col_ids = lax.broadcasted_iota(jnp.int32, (rows, slots), 1)

    def mask(h, carry):
        for j in range(per_dev):
            ones = jnp.where(col_ids < scalars[h ^ scalars[IRREPS + j]], 1.0, 0.0)
            cols = ones.astype(jnp.bfloat16)
            for owner in range(blk_count):
                keep = cols
                if (owner + 1) * rows > slots // 2:
                    in_rows = row_ids < scalars[h] - owner * rows
                    keep = jnp.where(in_rows, ones, 0.0).astype(jnp.bfloat16)
                block = piece_ref[owner, j, h] * keep
                at = slice(owner * rows, (owner + 1) * rows)
                if whole_tiles:
                    masked_ref[j, h, at, :] = block
                else:
                    assembled[at, :] = block.astype(jnp.float32)
            if not whole_tiles:
                masked_ref[j, h] = assembled[...].astype(jnp.bfloat16)
        return carry

    lax.fori_loop(0, IRREPS, mask, 0, unroll=2)
    slab_refs = join_parts(part_counts, part_refs, joined)
    add_slabs(scalars, slab_at, slab_refs, masked_ref, ladder_ref, None)


def second_kernel(slab_at, part_counts, scalars, masked_ref, before_ref, *refs):
    part_refs, (ladder_ref, joined) = refs[:-2], refs[-2:]
    slab_refs = join_parts(part_counts, part_refs, joined)
    add_slabs(scalars, slab_at, slab_refs, masked_ref, ladder_ref, before_ref)


def ladder_call(kernel, slab_at, scalars, inputs, slabs, per_dev, slots):
    vmem = pl.BlockSpec(memory_space=pltpu.VMEM)
    parts = [part for slab in slabs for part in slab]
    part_counts = [len(slab) for slab in slabs]
    rooms = max(1, sum(count > 1 for count in part_counts))
    blocks = (per_dev, IRREPS, slots, slots)
    ladder_shape = jax.ShapeDtypeStruct(blocks, jnp.float32)
    joined = pltpu.VMEM((rooms, IRREPS, slots, slots), jnp.bfloat16)
    first = kernel is first_kernel
    return pl.pallas_call(
        functools.partial(kernel, slab_at, part_counts),
        out_shape=[ladder_shape, jax.ShapeDtypeStruct(blocks, jnp.bfloat16)] if first else ladder_shape,
        in_specs=[pl.BlockSpec(memory_space=pltpu.SMEM)] + [vmem] * (len(inputs) + len(parts)),
        out_specs=[vmem] * 2 if first else vmem,
        scratch_shapes=[pltpu.VMEM((slots, slots), jnp.float32), joined] if first else [joined],
        compiler_params=pltpu.CompilerParams(vmem_limit_bytes=16 * 1024 * 1024),
        cost_estimate=pl.CostEstimate(
            flops=per_dev * IRREPS * 2 * len(slabs) * 2 * slots**3,
            bytes_accessed=10 * 1024 * 1024,
            transcendentals=0,
        ),
    )(scalars, *inputs, *parts)


def dress_kernel(per_dev, planes, scalars, same_ref, other_ref, *refs):
    ladder_ref, masked_ref = refs[:2]
    out_refs, (coupling, total) = refs[2:-2], refs[-2:]
    blk_count = len(out_refs)
    _, _, rows, slots = out_refs[0].shape
    blk = lax.axis_index("blk")
    core = lax.axis_index("grp") % 2
    half = len(planes)
    for k, place in enumerate(plane_places(planes, IRREPS // lax.axis_size("grp"))):
        coupling[core * half + place] = same_ref[k]
        coupling[(1 - core) * half + place] = other_ref[k]
    row_ids = lax.broadcasted_iota(jnp.int32, (slots, slots), 0)
    col_ids = lax.broadcasted_iota(jnp.int32, (slots, slots), 1)

    def one_block(h, carry):
        for j in range(per_dev):
            col = h ^ scalars[IRREPS + j]
            block = masked_ref[j, h]
            acc = ladder_ref[j, h]
            acc += jnp.dot(block, coupling[col], preferred_element_type=jnp.float32)
            acc += jnp.dot(coupling[h], block, preferred_element_type=jnp.float32)
            keep = (row_ids < scalars[h]) & (col_ids < scalars[col])
            total[j] = jnp.where(keep, acc, 0.0)
            for s, out_ref in enumerate(out_refs):
                at = pl.ds(pl.multiple_of((blk ^ s) * rows, rows), rows)
                out_ref[j, h] = total[j, at, :].astype(jnp.bfloat16)
        return carry

    lax.fori_loop(0, IRREPS, one_block, 0, unroll=4)


def dress_call(scalars, planes, blk_count, ladder, masked, same_core, other_core):
    per_dev, slots = ladder.shape[0], same_core.shape[-1]
    vmem = pl.BlockSpec(memory_space=pltpu.VMEM)
    return pl.pallas_call(
        functools.partial(dress_kernel, per_dev, planes),
        out_shape=[
            jax.ShapeDtypeStruct((per_dev, IRREPS, slots // blk_count, slots), jnp.bfloat16)
        ]
        * blk_count,
        in_specs=[pl.BlockSpec(memory_space=pltpu.SMEM)] + [vmem] * 4,
        out_specs=[vmem] * blk_count,
        scratch_shapes=[
            pltpu.VMEM((IRREPS, slots, slots), jnp.bfloat16),
            pltpu.VMEM((per_dev, slots, slots), jnp.float32),
        ],
        compiler_params=pltpu.CompilerParams(vmem_limit_bytes=16 * 1024 * 1024),
        cost_estimate=pl.CostEstimate(
            flops=per_dev * IRREPS * 4 * slots**3, bytes_accessed=8 * 1024 * 1024, transcendentals=0
        ),
    )(scalars, same_core, other_core, ladder, masked)


def after(value, *others):
    return lax.optimization_barrier((value, *others))[0]


def plane_places(planes, low_count):
    x, low = lax.axis_index("grp") // 2, lax.axis_index("blk") % low_count
    return [(x ^ dx) * low_count + (low ^ dy) for dx, dy in planes]


def factor_kernel(planes, low_count, kept, came, *out_refs):
    dims = (((0,), (0,)), ((), ()))
    for h, out_ref in zip(plane_places(planes, low_count), out_refs):
        total = lax.dot_general(kept[h, 0], kept[h, 1], dims, preferred_element_type=jnp.float32)
        total += lax.dot_general(came[h, 0], came[h, 1], dims, preferred_element_type=jnp.float32)
        out_ref[...] = total.astype(out_ref.dtype)


def plane_permute(value, grp_count, blk_count, dx, dy):
    perm = [
        (g * blk_count + b, (g ^ (2 * dx)) * blk_count + (b ^ dy))
        for g in range(grp_count)
        for b in range(blk_count)
    ]
    return lax.ppermute(value, ("grp", "blk"), perm)


def per_device(amplitudes, chol_vv, chol_irrep, pair_occ, occ_irrep, vir_count, ov_left, ov_right):
    blk_count = lax.axis_size("blk")
    grp_count = lax.axis_size("grp")
    pair_total, _, rows, slots = amplitudes.shape
    per_dev = pair_total // blk_count
    grp, blk = lax.axis_index("grp"), lax.axis_index("blk")

    by_dest = amplitudes.reshape(blk_count, per_dev, IRREPS, rows, slots)
    all_rows = lax.all_to_all(by_dest, "blk", split_axis=0, concat_axis=0, tiled=True)

    ov_rows = ov_left.shape[0]
    low_count = IRREPS // grp_count
    core, x, low = grp % 2, grp // 2, blk % low_count
    planes = [(dx, dy) for dx in range(grp_count // 2) for dy in range(low_count)]
    half = len(planes)
    factors = jnp.stack([ov_left, ov_right]).transpose(2, 0, 1, 3)
    kept = lax.dynamic_slice_in_dim(factors, core * half, half, 0)
    away = lax.dynamic_slice_in_dim(factors, (1 - core) * half, half, 0)
    came = xor_permute(away, "grp", grp_count, 1)
    vmem = pl.BlockSpec(memory_space=pltpu.VMEM)
    local = pl.pallas_call(
        functools.partial(factor_kernel, planes, low_count),
        out_shape=[jax.ShapeDtypeStruct((slots, slots), jnp.bfloat16)] * half,
        in_specs=[vmem] * 2,
        out_specs=[vmem] * half,
        compiler_params=pltpu.CompilerParams(vmem_limit_bytes=8 * 1024 * 1024),
    )(kept, came)
    per_slab = chol_vv.shape[0]
    cut = IRREPS // 2

    def along_x(part):
        return [xor_permute(part, "grp", grp_count, 2 * s) for s in range(1, grp_count // 2)]

    def other_core_of(parts):
        return [xor_permute(part, "grp", grp_count, 1) for part in parts]

    first_half = along_x(chol_vv[:, :cut])

    parts = []
    for (dx, dy), part in zip(planes, local):
        if dx or dy:
            part = plane_permute(part, grp_count, blk_count, dx, dy)
        parts.append(part.astype(jnp.float32))
    total = sum(parts)
    total = after(total, *first_half)
    second_half = along_x(after(chol_vv[:, cut:], total))
    same = [(chol_vv,)] + list(zip(first_half, second_half))
    own_other = other_core_of([chol_vv])
    other = [(own_other[0],)]
    for one, two in zip(first_half, second_half):
        mid = two.shape[1] // 2
        other.append(tuple(other_core_of([one, two[:, :mid], two[:, mid:]])))

    slabs, owners = [], []
    for s in range(grp_count // 2):
        for c, group in enumerate((same, other)):
            for k in range(per_slab):
                slabs.append([part[k] for part in group[s]])
                owners.append((grp ^ (2 * s + c)) * per_slab + k)
    slab_irreps = chol_irrep[jnp.stack(owners)]

    pair_start = (grp * blk_count + blk) * per_dev
    own_pairs = lax.dynamic_slice_in_dim(pair_occ, pair_start, per_dev, 0)
    occ_ids = jnp.arange(occ_irrep.shape[0], dtype=jnp.int32)
    one_hot = own_pairs[:, :, None] == occ_ids[None, None, :]
    labels = jnp.sum(jnp.where(one_hot, occ_irrep[None, None, :], 0), axis=2)
    pair_irrep = jnp.bitwise_xor(labels[:, 0], labels[:, 1])

    scalars = jnp.concatenate([vir_count, pair_irrep, slab_irreps])
    slab_at = IRREPS + per_dev
    split = 2 * per_slab
    ladder, masked = ladder_call(
        first_kernel, slab_at, scalars, [all_rows], slabs[:split], per_dev, slots
    )

    bit = low_count
    while bit < blk_count:
        came = xor_permute(total.astype(jnp.bfloat16), "blk", blk_count, bit)
        if 2 * bit >= blk_count:
            came, ladder, masked = lax.optimization_barrier((came, ladder, masked))
        total = total + came.astype(jnp.float32)
        bit *= 2
    scale = 1.0 / math.sqrt(ov_rows * grp_count * blk_count)
    block = (total * scale).astype(jnp.bfloat16)
    got = [
        plane_permute(block, grp_count, blk_count, dx, dy) if dx or dy else block
        for dx, dy in planes
    ]
    if slabs[split:]:
        ladder = ladder_call(
            second_kernel, slab_at + split, scalars, [masked, ladder], slabs[split:], per_dev, slots
        )
    got, ladder = lax.optimization_barrier((tuple(got), ladder))
    same_core = jnp.stack(got)
    other_core = xor_permute(same_core, "grp", grp_count, 1)
    sent = dress_call(scalars, planes, blk_count, ladder, masked, same_core, other_core)
    result = jnp.zeros(amplitudes.shape, jnp.bfloat16)
    result = lax.dynamic_update_slice(result, sent[0], (blk * per_dev, 0, 0, 0))
    top = blk_count // 2
    far, near = list(range(blk_count - 1, top - 1, -1)), list(range(top - 1, 0, -1))
    for s in [s for two in zip(far, near + [0]) for s in two if s]:
        came = xor_permute(sent[s], "blk", blk_count, s)
        result = lax.dynamic_update_slice(result, came, ((blk ^ s) * per_dev, 0, 0, 0))
    return result


def solution(mesh):
    return jax.shard_map(
        per_device,
        mesh=mesh,
        in_specs=(
            P("grp", None, "blk", None),
            P("grp", None, None, None),
            P(),
            P(),
            P(),
            P(),
            P(("grp", "blk"), None, None),
            P(("grp", "blk"), None, None),
        ),
        out_specs=P("grp", None, "blk", None),
        check_vma=False,
    )
```

```python
import functools
import math

import jax
import jax.numpy as jnp
from jax import lax
from jax.experimental import pallas as pl
from jax.experimental.pallas import tpu as pltpu
from jax.sharding import PartitionSpec as P

IRREPS = 8


def xor_permute(value, axis, count, bits):
    return lax.ppermute(value, axis, [(i, i ^ bits) for i in range(count)])


def join_parts(part_counts, part_refs, joined):
    slab_refs, at, room = [], 0, 0
    for parts in part_counts:
        if parts == 1:
            slab_refs.append(part_refs[at])
        else:
            begin = 0
            for part in part_refs[at : at + parts]:
                joined[room, begin : begin + part.shape[0]] = part[...]
                begin += part.shape[0]
            slab_refs.append(joined.at[room])
            room += 1
        at += parts
    return slab_refs


def add_slabs(scalars, slab_at, slab_refs, masked_ref, ladder_ref, before_ref):
    per_dev = masked_ref.shape[0]

    def one_block(h, carry):
        for j in range(per_dev):
            col = h ^ scalars[IRREPS + j]
            halves = []
            for q, slab in enumerate(slab_refs):
                shift = scalars[slab_at + q]
                half = jnp.dot(
                    slab[h], masked_ref[j, h ^ shift], preferred_element_type=jnp.float32
                )
                halves.append(half.astype(jnp.bfloat16))
            acc = lax.dot_general(
                jnp.concatenate(halves, axis=1),
                jnp.concatenate([slab[col] for slab in slab_refs], axis=1),
                (((1,), (1,)), ((), ())),
                preferred_element_type=jnp.float32,
            )
            if before_ref is not None:
                acc += before_ref[j, h]
            ladder_ref[j, h] = acc
        return carry

    lax.fori_loop(0, IRREPS, one_block, 0, unroll=max(1, 32 // (per_dev * len(slab_refs))))


def first_kernel(slab_at, part_counts, scalars, piece_ref, *refs):
    part_refs, (ladder_ref, masked_ref, assembled, joined) = refs[:-4], refs[-4:]
    blk_count, per_dev, _, rows, slots = piece_ref.shape
    whole_tiles = rows % 16 == 0
    row_ids = lax.broadcasted_iota(jnp.int32, (rows, slots), 0)
    col_ids = lax.broadcasted_iota(jnp.int32, (rows, slots), 1)

    def mask(h, carry):
        for j in range(per_dev):
            ones = jnp.where(col_ids < scalars[h ^ scalars[IRREPS + j]], 1.0, 0.0)
            cols = ones.astype(jnp.bfloat16)
            for owner in range(blk_count):
                keep = cols
                if (owner + 1) * rows > slots // 2:
                    in_rows = row_ids < scalars[h] - owner * rows
                    keep = jnp.where(in_rows, ones, 0.0).astype(jnp.bfloat16)
                block = piece_ref[owner, j, h] * keep
                at = slice(owner * rows, (owner + 1) * rows)
                if whole_tiles:
                    masked_ref[j, h, at, :] = block
                else:
                    assembled[at, :] = block.astype(jnp.float32)
            if not whole_tiles:
                masked_ref[j, h] = assembled[...].astype(jnp.bfloat16)
        return carry

    lax.fori_loop(0, IRREPS, mask, 0, unroll=2)
    slab_refs = join_parts(part_counts, part_refs, joined)
    add_slabs(scalars, slab_at, slab_refs, masked_ref, ladder_ref, None)


def second_kernel(slab_at, part_counts, scalars, masked_ref, before_ref, *refs):
    part_refs, (ladder_ref, joined) = refs[:-2], refs[-2:]
    slab_refs = join_parts(part_counts, part_refs, joined)
    add_slabs(scalars, slab_at, slab_refs, masked_ref, ladder_ref, before_ref)


def ladder_call(kernel, slab_at, scalars, inputs, slabs, per_dev, slots):
    vmem = pl.BlockSpec(memory_space=pltpu.VMEM)
    parts = [part for slab in slabs for part in slab]
    part_counts = [len(slab) for slab in slabs]
    rooms = max(1, sum(count > 1 for count in part_counts))
    blocks = (per_dev, IRREPS, slots, slots)
    ladder_shape = jax.ShapeDtypeStruct(blocks, jnp.float32)
    joined = pltpu.VMEM((rooms, IRREPS, slots, slots), jnp.bfloat16)
    first = kernel is first_kernel
    return pl.pallas_call(
        functools.partial(kernel, slab_at, part_counts),
        out_shape=[ladder_shape, jax.ShapeDtypeStruct(blocks, jnp.bfloat16)] if first else ladder_shape,
        in_specs=[pl.BlockSpec(memory_space=pltpu.SMEM)] + [vmem] * (len(inputs) + len(parts)),
        out_specs=[vmem] * 2 if first else vmem,
        scratch_shapes=[pltpu.VMEM((slots, slots), jnp.float32), joined] if first else [joined],
        compiler_params=pltpu.CompilerParams(vmem_limit_bytes=16 * 1024 * 1024),
        cost_estimate=pl.CostEstimate(
            flops=per_dev * IRREPS * 2 * len(slabs) * 2 * slots**3,
            bytes_accessed=10 * 1024 * 1024,
            transcendentals=0,
        ),
    )(scalars, *inputs, *parts)


def dress_kernel(per_dev, planes, scalars, same_ref, other_ref, *refs):
    ladder_ref, masked_ref = refs[:2]
    out_refs, (coupling, total) = refs[2:-2], refs[-2:]
    blk_count = len(out_refs)
    _, _, rows, slots = out_refs[0].shape
    blk = lax.axis_index("blk")
    core = lax.axis_index("grp") % 2
    half = len(planes)
    for k, place in enumerate(plane_places(planes, IRREPS // lax.axis_size("grp"))):
        coupling[core * half + place] = same_ref[k]
        coupling[(1 - core) * half + place] = other_ref[k]
    row_ids = lax.broadcasted_iota(jnp.int32, (slots, slots), 0)
    col_ids = lax.broadcasted_iota(jnp.int32, (slots, slots), 1)

    def one_block(h, carry):
        for j in range(per_dev):
            col = h ^ scalars[IRREPS + j]
            block = masked_ref[j, h]
            acc = ladder_ref[j, h]
            acc += jnp.dot(
                jnp.concatenate([block, coupling[h]], axis=1),
                jnp.concatenate([coupling[col], block], axis=0),
                preferred_element_type=jnp.float32,
            )
            keep = (row_ids < scalars[h]) & (col_ids < scalars[col])
            total[j] = jnp.where(keep, acc, 0.0)
            for s, out_ref in enumerate(out_refs):
                at = pl.ds(pl.multiple_of((blk ^ s) * rows, rows), rows)
                out_ref[j, h] = total[j, at, :].astype(jnp.bfloat16)
        return carry

    lax.fori_loop(0, IRREPS, one_block, 0, unroll=4)


def dress_call(scalars, planes, blk_count, ladder, masked, same_core, other_core):
    per_dev, slots = ladder.shape[0], same_core.shape[-1]
    vmem = pl.BlockSpec(memory_space=pltpu.VMEM)
    return pl.pallas_call(
        functools.partial(dress_kernel, per_dev, planes),
        out_shape=[
            jax.ShapeDtypeStruct((per_dev, IRREPS, slots // blk_count, slots), jnp.bfloat16)
        ]
        * blk_count,
        in_specs=[pl.BlockSpec(memory_space=pltpu.SMEM)] + [vmem] * 4,
        out_specs=[vmem] * blk_count,
        scratch_shapes=[
            pltpu.VMEM((IRREPS, slots, slots), jnp.bfloat16),
            pltpu.VMEM((per_dev, slots, slots), jnp.float32),
        ],
        compiler_params=pltpu.CompilerParams(vmem_limit_bytes=16 * 1024 * 1024),
        cost_estimate=pl.CostEstimate(
            flops=per_dev * IRREPS * 4 * slots**3, bytes_accessed=8 * 1024 * 1024, transcendentals=0
        ),
    )(scalars, same_core, other_core, ladder, masked)


def after(value, *others):
    return lax.optimization_barrier((value, *others))[0]


def plane_places(planes, low_count):
    x, low = lax.axis_index("grp") // 2, lax.axis_index("blk") % low_count
    return [(x ^ dx) * low_count + (low ^ dy) for dx, dy in planes]


def factor_kernel(planes, low_count, kept, came, *out_refs):
    dims = (((0,), (0,)), ((), ()))
    for h, out_ref in zip(plane_places(planes, low_count), out_refs):
        total = lax.dot_general(kept[h, 0], kept[h, 1], dims, preferred_element_type=jnp.float32)
        total += lax.dot_general(came[h, 0], came[h, 1], dims, preferred_element_type=jnp.float32)
        out_ref[...] = total.astype(out_ref.dtype)


def plane_permute(value, grp_count, blk_count, dx, dy):
    perm = [
        (g * blk_count + b, (g ^ (2 * dx)) * blk_count + (b ^ dy))
        for g in range(grp_count)
        for b in range(blk_count)
    ]
    return lax.ppermute(value, ("grp", "blk"), perm)


def per_device(amplitudes, chol_vv, chol_irrep, pair_occ, occ_irrep, vir_count, ov_left, ov_right):
    blk_count = lax.axis_size("blk")
    grp_count = lax.axis_size("grp")
    pair_total, _, rows, slots = amplitudes.shape
    per_dev = pair_total // blk_count
    grp, blk = lax.axis_index("grp"), lax.axis_index("blk")

    by_dest = amplitudes.reshape(blk_count, per_dev, IRREPS, rows, slots)
    all_rows = lax.all_to_all(by_dest, "blk", split_axis=0, concat_axis=0, tiled=True)

    ov_rows = ov_left.shape[0]
    low_count = IRREPS // grp_count
    core, x, low = grp % 2, grp // 2, blk % low_count
    planes = [(dx, dy) for dx in range(grp_count // 2) for dy in range(low_count)]
    half = len(planes)
    factors = jnp.stack([ov_left, ov_right]).transpose(2, 0, 1, 3)
    kept = lax.dynamic_slice_in_dim(factors, core * half, half, 0)
    away = lax.dynamic_slice_in_dim(factors, (1 - core) * half, half, 0)
    came = xor_permute(away, "grp", grp_count, 1)
    vmem = pl.BlockSpec(memory_space=pltpu.VMEM)
    local = pl.pallas_call(
        functools.partial(factor_kernel, planes, low_count),
        out_shape=[jax.ShapeDtypeStruct((slots, slots), jnp.bfloat16)] * half,
        in_specs=[vmem] * 2,
        out_specs=[vmem] * half,
        compiler_params=pltpu.CompilerParams(vmem_limit_bytes=8 * 1024 * 1024),
    )(kept, came)
    per_slab = chol_vv.shape[0]
    cut = IRREPS // 2

    def along_x(part):
        return [xor_permute(part, "grp", grp_count, 2 * s) for s in range(1, grp_count // 2)]

    def other_core_of(parts):
        return [xor_permute(part, "grp", grp_count, 1) for part in parts]

    first_half = along_x(chol_vv[:, :cut])

    parts = []
    for (dx, dy), part in zip(planes, local):
        if dx or dy:
            part = plane_permute(part, grp_count, blk_count, dx, dy)
        parts.append(part.astype(jnp.float32))
    total = sum(parts)
    total = after(total, *first_half)
    second_half = along_x(after(chol_vv[:, cut:], total))
    same = [(chol_vv,)] + list(zip(first_half, second_half))
    own_other = other_core_of([chol_vv])
    other = [(own_other[0],)]
    for one, two in zip(first_half, second_half):
        mid = two.shape[1] // 2
        other.append(tuple(other_core_of([one, two[:, :mid], two[:, mid:]])))

    slabs, owners = [], []
    for s in range(grp_count // 2):
        for c, group in enumerate((same, other)):
            for k in range(per_slab):
                slabs.append([part[k] for part in group[s]])
                owners.append((grp ^ (2 * s + c)) * per_slab + k)
    slab_irreps = chol_irrep[jnp.stack(owners)]

    pair_start = (grp * blk_count + blk) * per_dev
    own_pairs = lax.dynamic_slice_in_dim(pair_occ, pair_start, per_dev, 0)
    occ_ids = jnp.arange(occ_irrep.shape[0], dtype=jnp.int32)
    one_hot = own_pairs[:, :, None] == occ_ids[None, None, :]
    labels = jnp.sum(jnp.where(one_hot, occ_irrep[None, None, :], 0), axis=2)
    pair_irrep = jnp.bitwise_xor(labels[:, 0], labels[:, 1])

    scalars = jnp.concatenate([vir_count, pair_irrep, slab_irreps])
    slab_at = IRREPS + per_dev
    split = 2 * per_slab

    bit = low_count
    while bit < blk_count:
        sent = total.astype(jnp.bfloat16)
        if 2 * bit >= blk_count:
            sent, all_rows = lax.optimization_barrier((sent, all_rows))
        came = xor_permute(sent, "blk", blk_count, bit)
        if 2 * bit >= blk_count:
            ladder, masked = ladder_call(
                first_kernel, slab_at, scalars, [all_rows], slabs[:split], per_dev, slots
            )
            came, ladder, masked = lax.optimization_barrier((came, ladder, masked))
        total = total + came.astype(jnp.float32)
        bit *= 2
    scale = 1.0 / math.sqrt(ov_rows * grp_count * blk_count)
    block = (total * scale).astype(jnp.bfloat16)
    got = [
        plane_permute(block, grp_count, blk_count, dx, dy) if dx or dy else block
        for dx, dy in planes
    ]
    if slabs[split:]:
        ladder = ladder_call(
            second_kernel, slab_at + split, scalars, [masked, ladder], slabs[split:], per_dev, slots
        )
    got, ladder = lax.optimization_barrier((tuple(got), ladder))
    same_core = jnp.stack(got)
    other_core = xor_permute(same_core, "grp", grp_count, 1)
    sent = dress_call(scalars, planes, blk_count, ladder, masked, same_core, other_core)
    result = jnp.zeros(amplitudes.shape, jnp.bfloat16)
    result = lax.dynamic_update_slice(result, sent[0], (blk * per_dev, 0, 0, 0))
    top = blk_count // 2
    far, near = list(range(top, blk_count)), list(range(1, top))
    for s in [s for two in zip(far, near + [0]) for s in two if s]:
        came = xor_permute(sent[s], "blk", blk_count, s)
        result = lax.dynamic_update_slice(result, came, ((blk ^ s) * per_dev, 0, 0, 0))
    return result


def solution(mesh):
    return jax.shard_map(
        per_device,
        mesh=mesh,
        in_specs=(
            P("grp", None, "blk", None),
            P("grp", None, None, None),
            P(),
            P(),
            P(),
            P(),
            P(("grp", "blk"), None, None),
            P(("grp", "blk"), None, None),
        ),
        out_specs=P("grp", None, "blk", None),
        check_vma=False,
    )
```

```python
import functools
import math

import jax
import jax.numpy as jnp
from jax import lax
from jax.experimental import pallas as pl
from jax.experimental.pallas import tpu as pltpu
from jax.sharding import PartitionSpec as P

IRREPS = 8


def xor_permute(value, axis, count, bits):
    return lax.ppermute(value, axis, [(i, i ^ bits) for i in range(count)])


def join_parts(part_counts, part_refs, joined):
    slab_refs, at, room = [], 0, 0
    for parts in part_counts:
        if parts == 1:
            slab_refs.append(part_refs[at])
        else:
            begin = 0
            for part in part_refs[at : at + parts]:
                joined[room, begin : begin + part.shape[0]] = part[...]
                begin += part.shape[0]
            slab_refs.append(joined.at[room])
            room += 1
        at += parts
    return slab_refs


def add_slabs(scalars, slab_at, slab_refs, masked_ref, ladder_ref, before_ref):
    per_dev = masked_ref.shape[0]

    def one_block(h, carry):
        for j in range(per_dev):
            col = h ^ scalars[IRREPS + j]
            halves = []
            for q, slab in enumerate(slab_refs):
                shift = scalars[slab_at + q]
                half = jnp.dot(
                    slab[h], masked_ref[j, h ^ shift], preferred_element_type=jnp.float32
                )
                halves.append(half.astype(jnp.bfloat16))
            acc = lax.dot_general(
                jnp.concatenate(halves, axis=1),
                jnp.concatenate([slab[col] for slab in slab_refs], axis=1),
                (((1,), (1,)), ((), ())),
                preferred_element_type=jnp.float32,
            )
            if before_ref is not None:
                acc += before_ref[j, h]
            ladder_ref[j, h] = acc
        return carry

    lax.fori_loop(0, IRREPS, one_block, 0, unroll=max(1, 32 // (per_dev * len(slab_refs))))


def first_kernel(slab_at, part_counts, scalars, piece_ref, *refs):
    part_refs, (ladder_ref, masked_ref, assembled, joined) = refs[:-4], refs[-4:]
    blk_count, per_dev, _, rows, slots = piece_ref.shape
    whole_tiles = rows % 16 == 0
    row_ids = lax.broadcasted_iota(jnp.int32, (rows, slots), 0)
    col_ids = lax.broadcasted_iota(jnp.int32, (rows, slots), 1)

    def mask(h, carry):
        for j in range(per_dev):
            ones = jnp.where(col_ids < scalars[h ^ scalars[IRREPS + j]], 1.0, 0.0)
            cols = ones.astype(jnp.bfloat16)
            for owner in range(blk_count):
                keep = cols
                if (owner + 1) * rows > slots // 2:
                    in_rows = row_ids < scalars[h] - owner * rows
                    keep = jnp.where(in_rows, ones, 0.0).astype(jnp.bfloat16)
                block = piece_ref[owner, j, h] * keep
                at = slice(owner * rows, (owner + 1) * rows)
                if whole_tiles:
                    masked_ref[j, h, at, :] = block
                else:
                    assembled[at, :] = block.astype(jnp.float32)
            if not whole_tiles:
                masked_ref[j, h] = assembled[...].astype(jnp.bfloat16)
        return carry

    lax.fori_loop(0, IRREPS, mask, 0, unroll=2)
    slab_refs = join_parts(part_counts, part_refs, joined)
    add_slabs(scalars, slab_at, slab_refs, masked_ref, ladder_ref, None)


def second_kernel(slab_at, part_counts, scalars, masked_ref, before_ref, *refs):
    part_refs, (ladder_ref, joined) = refs[:-2], refs[-2:]
    slab_refs = join_parts(part_counts, part_refs, joined)
    add_slabs(scalars, slab_at, slab_refs, masked_ref, ladder_ref, before_ref)


def ladder_call(kernel, slab_at, scalars, inputs, slabs, per_dev, slots):
    vmem = pl.BlockSpec(memory_space=pltpu.VMEM)
    parts = [part for slab in slabs for part in slab]
    part_counts = [len(slab) for slab in slabs]
    rooms = max(1, sum(count > 1 for count in part_counts))
    blocks = (per_dev, IRREPS, slots, slots)
    ladder_shape = jax.ShapeDtypeStruct(blocks, jnp.float32)
    joined = pltpu.VMEM((rooms, IRREPS, slots, slots), jnp.bfloat16)
    first = kernel is first_kernel
    return pl.pallas_call(
        functools.partial(kernel, slab_at, part_counts),
        out_shape=[ladder_shape, jax.ShapeDtypeStruct(blocks, jnp.bfloat16)] if first else ladder_shape,
        in_specs=[pl.BlockSpec(memory_space=pltpu.SMEM)] + [vmem] * (len(inputs) + len(parts)),
        out_specs=[vmem] * 2 if first else vmem,
        scratch_shapes=[pltpu.VMEM((slots, slots), jnp.float32), joined] if first else [joined],
        compiler_params=pltpu.CompilerParams(vmem_limit_bytes=16 * 1024 * 1024),
        cost_estimate=pl.CostEstimate(
            flops=per_dev * IRREPS * 2 * len(slabs) * 2 * slots**3,
            bytes_accessed=10 * 1024 * 1024,
            transcendentals=0,
        ),
    )(scalars, *inputs, *parts)


def dress_kernel(per_dev, planes, scalars, same_ref, other_ref, *refs):
    ladder_ref, masked_ref = refs[:2]
    out_refs, (coupling, total) = refs[2:-2], refs[-2:]
    blk_count = len(out_refs)
    _, _, rows, slots = out_refs[0].shape
    blk = lax.axis_index("blk")
    core = lax.axis_index("grp") % 2
    half = len(planes)
    for k, place in enumerate(plane_places(planes, IRREPS // lax.axis_size("grp"))):
        coupling[core * half + place] = same_ref[k]
        coupling[(1 - core) * half + place] = other_ref[k]
    row_ids = lax.broadcasted_iota(jnp.int32, (slots, slots), 0)
    col_ids = lax.broadcasted_iota(jnp.int32, (slots, slots), 1)

    def one_block(h, carry):
        for j in range(per_dev):
            col = h ^ scalars[IRREPS + j]
            block = masked_ref[j, h]
            acc = ladder_ref[j, h]
            acc += jnp.dot(
                jnp.concatenate([block, coupling[h]], axis=1),
                jnp.concatenate([coupling[col], block], axis=0),
                preferred_element_type=jnp.float32,
            )
            keep = (row_ids < scalars[h]) & (col_ids < scalars[col])
            total[j] = jnp.where(keep, acc, 0.0).astype(total.dtype)
            for s, out_ref in enumerate(out_refs):
                at = pl.ds(pl.multiple_of((blk ^ s) * rows, rows), rows)
                out_ref[j, h] = total[j, at, :].astype(jnp.bfloat16)
        return carry

    lax.fori_loop(0, IRREPS, one_block, 0, unroll=8)


def dress_call(scalars, planes, blk_count, ladder, masked, same_core, other_core):
    per_dev, slots = ladder.shape[0], same_core.shape[-1]
    vmem = pl.BlockSpec(memory_space=pltpu.VMEM)
    return pl.pallas_call(
        functools.partial(dress_kernel, per_dev, planes),
        out_shape=[
            jax.ShapeDtypeStruct((per_dev, IRREPS, slots // blk_count, slots), jnp.bfloat16)
        ]
        * blk_count,
        in_specs=[pl.BlockSpec(memory_space=pltpu.SMEM)] + [vmem] * 4,
        out_specs=[vmem] * blk_count,
        scratch_shapes=[
            pltpu.VMEM((IRREPS, slots, slots), jnp.bfloat16),
            pltpu.VMEM(
                (per_dev, slots, slots), jnp.float32 if slots // blk_count % 16 else jnp.bfloat16
            ),
        ],
        compiler_params=pltpu.CompilerParams(vmem_limit_bytes=16 * 1024 * 1024),
        cost_estimate=pl.CostEstimate(
            flops=per_dev * IRREPS * 4 * slots**3, bytes_accessed=8 * 1024 * 1024, transcendentals=0
        ),
    )(scalars, same_core, other_core, ladder, masked)


def after(value, *others):
    return lax.optimization_barrier((value, *others))[0]


def plane_places(planes, low_count):
    x, low = lax.axis_index("grp") // 2, lax.axis_index("blk") % low_count
    return [(x ^ dx) * low_count + (low ^ dy) for dx, dy in planes]


def factor_kernel(planes, low_count, kept, came, *out_refs):
    dims = (((0,), (0,)), ((), ()))
    for h, out_ref in zip(plane_places(planes, low_count), out_refs):
        total = lax.dot_general(kept[h, 0], kept[h, 1], dims, preferred_element_type=jnp.float32)
        total += lax.dot_general(came[h, 0], came[h, 1], dims, preferred_element_type=jnp.float32)
        out_ref[...] = total.astype(out_ref.dtype)


def plane_permute(value, grp_count, blk_count, dx, dy):
    perm = [
        (g * blk_count + b, (g ^ (2 * dx)) * blk_count + (b ^ dy))
        for g in range(grp_count)
        for b in range(blk_count)
    ]
    return lax.ppermute(value, ("grp", "blk"), perm)


def per_device(amplitudes, chol_vv, chol_irrep, pair_occ, occ_irrep, vir_count, ov_left, ov_right):
    blk_count = lax.axis_size("blk")
    grp_count = lax.axis_size("grp")
    pair_total, _, rows, slots = amplitudes.shape
    per_dev = pair_total // blk_count
    grp, blk = lax.axis_index("grp"), lax.axis_index("blk")

    by_dest = amplitudes.reshape(blk_count, per_dev, IRREPS, rows, slots)
    all_rows = lax.all_to_all(by_dest, "blk", split_axis=0, concat_axis=0, tiled=True)

    ov_rows = ov_left.shape[0]
    low_count = IRREPS // grp_count
    core, x, low = grp % 2, grp // 2, blk % low_count
    planes = [(dx, dy) for dx in range(grp_count // 2) for dy in range(low_count)]
    half = len(planes)
    factors = jnp.stack([ov_left, ov_right]).transpose(2, 0, 1, 3)
    kept = lax.dynamic_slice_in_dim(factors, core * half, half, 0)
    away = lax.dynamic_slice_in_dim(factors, (1 - core) * half, half, 0)
    came = xor_permute(away, "grp", grp_count, 1)
    vmem = pl.BlockSpec(memory_space=pltpu.VMEM)
    local = pl.pallas_call(
        functools.partial(factor_kernel, planes, low_count),
        out_shape=[jax.ShapeDtypeStruct((slots, slots), jnp.bfloat16)] * half,
        in_specs=[vmem] * 2,
        out_specs=[vmem] * half,
        compiler_params=pltpu.CompilerParams(vmem_limit_bytes=8 * 1024 * 1024),
    )(kept, came)
    per_slab = chol_vv.shape[0]
    cut = IRREPS // 2

    def along_x(part):
        return [xor_permute(part, "grp", grp_count, 2 * s) for s in range(1, grp_count // 2)]

    def other_core_of(parts):
        return [xor_permute(part, "grp", grp_count, 1) for part in parts]

    first_half = along_x(chol_vv[:, :cut])

    parts = []
    for (dx, dy), part in zip(planes, local):
        if dx or dy:
            part = plane_permute(part, grp_count, blk_count, dx, dy)
        parts.append(part.astype(jnp.float32))
    total = sum(parts)
    total = after(total, *first_half)
    second_half = along_x(after(chol_vv[:, cut:], total))
    same = [(chol_vv,)] + list(zip(first_half, second_half))
    own_other = other_core_of([chol_vv])
    other = [(own_other[0],)]
    for one, two in zip(first_half, second_half):
        mid = two.shape[1] // 2
        other.append(tuple(other_core_of([one, two[:, :mid], two[:, mid:]])))

    slabs, owners = [], []
    for s in range(grp_count // 2):
        for c, group in enumerate((same, other)):
            for k in range(per_slab):
                slabs.append([part[k] for part in group[s]])
                owners.append((grp ^ (2 * s + c)) * per_slab + k)
    slab_irreps = chol_irrep[jnp.stack(owners)]

    pair_start = (grp * blk_count + blk) * per_dev
    own_pairs = lax.dynamic_slice_in_dim(pair_occ, pair_start, per_dev, 0)
    occ_ids = jnp.arange(occ_irrep.shape[0], dtype=jnp.int32)
    one_hot = own_pairs[:, :, None] == occ_ids[None, None, :]
    labels = jnp.sum(jnp.where(one_hot, occ_irrep[None, None, :], 0), axis=2)
    pair_irrep = jnp.bitwise_xor(labels[:, 0], labels[:, 1])

    scalars = jnp.concatenate([vir_count, pair_irrep, slab_irreps])
    slab_at = IRREPS + per_dev
    split = 2 * per_slab

    bit = low_count
    while bit < blk_count:
        sent = total.astype(jnp.bfloat16)
        if 2 * bit >= blk_count:
            sent, all_rows = lax.optimization_barrier((sent, all_rows))
        came = xor_permute(sent, "blk", blk_count, bit)
        if 2 * bit >= blk_count:
            ladder, masked = ladder_call(
                first_kernel, slab_at, scalars, [all_rows], slabs[:split], per_dev, slots
            )
            came, ladder, masked = lax.optimization_barrier((came, ladder, masked))
        total = total + came.astype(jnp.float32)
        bit *= 2
    scale = 1.0 / math.sqrt(ov_rows * grp_count * blk_count)
    block = (total * scale).astype(jnp.bfloat16)
    got = [
        plane_permute(block, grp_count, blk_count, dx, dy) if dx or dy else block
        for dx, dy in planes
    ]
    if slabs[split:]:
        ladder = ladder_call(
            second_kernel, slab_at + split, scalars, [masked, ladder], slabs[split:], per_dev, slots
        )
    got, ladder = lax.optimization_barrier((tuple(got), ladder))
    same_core = jnp.stack(got)
    other_core = xor_permute(same_core, "grp", grp_count, 1)
    sent = dress_call(scalars, planes, blk_count, ladder, masked, same_core, other_core)
    result = jnp.zeros(amplitudes.shape, jnp.bfloat16)
    result = lax.dynamic_update_slice(result, sent[0], (blk * per_dev, 0, 0, 0))
    top = blk_count // 2
    far, near = list(range(top, blk_count)), list(range(1, top))
    for s in [s for two in zip(far, near + [0]) for s in two if s]:
        came = xor_permute(sent[s], "blk", blk_count, s)
        result = lax.dynamic_update_slice(result, came, ((blk ^ s) * per_dev, 0, 0, 0))
    return result


def solution(mesh):
    return jax.shard_map(
        per_device,
        mesh=mesh,
        in_specs=(
            P("grp", None, "blk", None),
            P("grp", None, None, None),
            P(),
            P(),
            P(),
            P(),
            P(("grp", "blk"), None, None),
            P(("grp", "blk"), None, None),
        ),
        out_specs=P("grp", None, "blk", None),
        check_vma=False,
    )
```

```python
import functools
import math

import jax
import jax.numpy as jnp
from jax import lax
from jax.experimental import pallas as pl
from jax.experimental.pallas import tpu as pltpu
from jax.sharding import PartitionSpec as P

IRREPS = 8


def xor_permute(value, axis, count, bits):
    return lax.ppermute(value, axis, [(i, i ^ bits) for i in range(count)])


def join_parts(part_counts, part_refs, joined):
    slab_refs, at, room = [], 0, 0
    for parts in part_counts:
        if parts == 1:
            slab_refs.append(part_refs[at])
        else:
            begin = 0
            for part in part_refs[at : at + parts]:
                joined[room, begin : begin + part.shape[0]] = part[...]
                begin += part.shape[0]
            slab_refs.append(joined.at[room])
            room += 1
        at += parts
    return slab_refs


def add_slabs(scalars, slab_at, slab_refs, masked_ref, ladder_ref, before_ref):
    per_dev = masked_ref.shape[0]

    def one_block(h, carry):
        for j in range(per_dev):
            col = h ^ scalars[IRREPS + j]
            halves = []
            for q, slab in enumerate(slab_refs):
                shift = scalars[slab_at + q]
                half = jnp.dot(
                    slab[h], masked_ref[j, h ^ shift], preferred_element_type=jnp.float32
                )
                halves.append(half.astype(jnp.bfloat16))
            acc = lax.dot_general(
                jnp.concatenate(halves, axis=1),
                jnp.concatenate([slab[col] for slab in slab_refs], axis=1),
                (((1,), (1,)), ((), ())),
                preferred_element_type=jnp.float32,
            )
            if before_ref is not None:
                acc += before_ref[j, h]
            ladder_ref[j, h] = acc
        return carry

    lax.fori_loop(0, IRREPS, one_block, 0, unroll=max(1, 32 // (per_dev * len(slab_refs))))


def first_kernel(slab_at, part_counts, scalars, piece_ref, *refs):
    part_refs, (ladder_ref, masked_ref, assembled, joined) = refs[:-4], refs[-4:]
    blk_count, per_dev, _, rows, slots = piece_ref.shape
    whole_tiles = rows % 16 == 0
    row_ids = lax.broadcasted_iota(jnp.int32, (rows, slots), 0)
    col_ids = lax.broadcasted_iota(jnp.int32, (rows, slots), 1)

    def mask(h, carry):
        for j in range(per_dev):
            ones = jnp.where(col_ids < scalars[h ^ scalars[IRREPS + j]], 1.0, 0.0)
            cols = ones.astype(jnp.bfloat16)
            for owner in range(blk_count):
                keep = cols
                if (owner + 1) * rows > slots // 2:
                    in_rows = row_ids < scalars[h] - owner * rows
                    keep = jnp.where(in_rows, ones, 0.0).astype(jnp.bfloat16)
                block = piece_ref[owner, j, h] * keep
                at = slice(owner * rows, (owner + 1) * rows)
                if whole_tiles:
                    masked_ref[j, h, at, :] = block
                else:
                    assembled[at, :] = block.astype(jnp.float32)
            if not whole_tiles:
                masked_ref[j, h] = assembled[...].astype(jnp.bfloat16)
        return carry

    lax.fori_loop(0, IRREPS, mask, 0, unroll=2)
    slab_refs = join_parts(part_counts, part_refs, joined)
    add_slabs(scalars, slab_at, slab_refs, masked_ref, ladder_ref, None)


def second_kernel(slab_at, part_counts, scalars, masked_ref, before_ref, *refs):
    part_refs, (ladder_ref, joined) = refs[:-2], refs[-2:]
    slab_refs = join_parts(part_counts, part_refs, joined)
    add_slabs(scalars, slab_at, slab_refs, masked_ref, ladder_ref, before_ref)


def ladder_call(kernel, slab_at, scalars, inputs, slabs, per_dev, slots):
    vmem = pl.BlockSpec(memory_space=pltpu.VMEM)
    parts = [part for slab in slabs for part in slab]
    part_counts = [len(slab) for slab in slabs]
    rooms = max(1, sum(count > 1 for count in part_counts))
    blocks = (per_dev, IRREPS, slots, slots)
    ladder_shape = jax.ShapeDtypeStruct(blocks, jnp.float32)
    joined = pltpu.VMEM((rooms, IRREPS, slots, slots), jnp.bfloat16)
    first = kernel is first_kernel
    return pl.pallas_call(
        functools.partial(kernel, slab_at, part_counts),
        out_shape=[ladder_shape, jax.ShapeDtypeStruct(blocks, jnp.bfloat16)] if first else ladder_shape,
        in_specs=[pl.BlockSpec(memory_space=pltpu.SMEM)] + [vmem] * (len(inputs) + len(parts)),
        out_specs=[vmem] * 2 if first else vmem,
        scratch_shapes=[pltpu.VMEM((slots, slots), jnp.float32), joined] if first else [joined],
        compiler_params=pltpu.CompilerParams(vmem_limit_bytes=16 * 1024 * 1024),
        cost_estimate=pl.CostEstimate(
            flops=per_dev * IRREPS * 2 * len(slabs) * 2 * slots**3,
            bytes_accessed=10 * 1024 * 1024,
            transcendentals=0,
        ),
    )(scalars, *inputs, *parts)


def dress_kernel(per_dev, planes, scalars, same_ref, other_ref, *refs):
    ladder_ref, masked_ref = refs[:2]
    out_refs, (coupling, total) = refs[2:-2], refs[-2:]
    blk_count = len(out_refs)
    _, _, rows, slots = out_refs[0].shape
    blk = lax.axis_index("blk")
    core = lax.axis_index("grp") % 2
    half = len(planes)
    for k, place in enumerate(plane_places(planes, IRREPS // lax.axis_size("grp"))):
        coupling[core * half + place] = same_ref[k]
        coupling[(1 - core) * half + place] = other_ref[k]
    row_ids = lax.broadcasted_iota(jnp.int32, (slots, slots), 0)
    col_ids = lax.broadcasted_iota(jnp.int32, (slots, slots), 1)

    def one_block(h, carry):
        for j in range(per_dev):
            col = h ^ scalars[IRREPS + j]
            block = masked_ref[j, h]
            acc = ladder_ref[j, h]
            acc += jnp.dot(
                jnp.concatenate([block, coupling[h]], axis=1),
                jnp.concatenate([coupling[col], block], axis=0),
                preferred_element_type=jnp.float32,
            )
            keep = (row_ids < scalars[h]) & (col_ids < scalars[col])
            total[j] = jnp.where(keep, acc, 0.0).astype(total.dtype)
            for s, out_ref in enumerate(out_refs):
                at = pl.ds(pl.multiple_of((blk ^ s) * rows, rows), rows)
                out_ref[j, h] = total[j, at, :].astype(jnp.bfloat16)
        return carry

    lax.fori_loop(0, IRREPS, one_block, 0, unroll=8)


def dress_call(scalars, planes, blk_count, ladder, masked, same_core, other_core):
    per_dev, slots = ladder.shape[0], same_core.shape[-1]
    vmem = pl.BlockSpec(memory_space=pltpu.VMEM)
    return pl.pallas_call(
        functools.partial(dress_kernel, per_dev, planes),
        out_shape=[
            jax.ShapeDtypeStruct((per_dev, IRREPS, slots // blk_count, slots), jnp.bfloat16)
        ]
        * blk_count,
        in_specs=[pl.BlockSpec(memory_space=pltpu.SMEM)] + [vmem] * 4,
        out_specs=[vmem] * blk_count,
        scratch_shapes=[
            pltpu.VMEM((IRREPS, slots, slots), jnp.bfloat16),
            pltpu.VMEM(
                (per_dev, slots, slots), jnp.float32 if slots // blk_count % 16 else jnp.bfloat16
            ),
        ],
        compiler_params=pltpu.CompilerParams(vmem_limit_bytes=16 * 1024 * 1024),
        cost_estimate=pl.CostEstimate(
            flops=per_dev * IRREPS * 4 * slots**3, bytes_accessed=8 * 1024 * 1024, transcendentals=0
        ),
    )(scalars, same_core, other_core, ladder, masked)


def after(value, *others):
    return lax.optimization_barrier((value, *others))[0]


def plane_places(planes, low_count):
    x, low = lax.axis_index("grp") // 2, lax.axis_index("blk") % low_count
    return [(x ^ dx) * low_count + (low ^ dy) for dx, dy in planes]


def factor_kernel(planes, low_count, kept, came, *out_refs):
    dims = (((0,), (0,)), ((), ()))
    for h, out_ref in zip(plane_places(planes, low_count), out_refs):
        total = lax.dot_general(kept[h, 0], kept[h, 1], dims, preferred_element_type=jnp.float32)
        total += lax.dot_general(came[h, 0], came[h, 1], dims, preferred_element_type=jnp.float32)
        out_ref[...] = total.astype(out_ref.dtype)


def plane_permute(value, grp_count, blk_count, dx, dy):
    perm = [
        (g * blk_count + b, (g ^ (2 * dx)) * blk_count + (b ^ dy))
        for g in range(grp_count)
        for b in range(blk_count)
    ]
    return lax.ppermute(value, ("grp", "blk"), perm)


def per_device(amplitudes, chol_vv, chol_irrep, pair_occ, occ_irrep, vir_count, ov_left, ov_right):
    blk_count = lax.axis_size("blk")
    grp_count = lax.axis_size("grp")
    pair_total, _, rows, slots = amplitudes.shape
    per_dev = pair_total // blk_count
    grp, blk = lax.axis_index("grp"), lax.axis_index("blk")

    by_dest = amplitudes.reshape(blk_count, per_dev, IRREPS, rows, slots)
    all_rows = lax.all_to_all(by_dest, "blk", split_axis=0, concat_axis=0, tiled=True)

    ov_rows = ov_left.shape[0]
    low_count = IRREPS // grp_count
    core, x, low = grp % 2, grp // 2, blk % low_count
    planes = [(dx, dy) for dx in range(grp_count // 2) for dy in range(low_count)]
    half = len(planes)
    factors = jnp.stack([ov_left, ov_right]).transpose(2, 0, 1, 3)
    kept = lax.dynamic_slice_in_dim(factors, core * half, half, 0)
    away = lax.dynamic_slice_in_dim(factors, (1 - core) * half, half, 0)
    came = xor_permute(away, "grp", grp_count, 1)
    vmem = pl.BlockSpec(memory_space=pltpu.VMEM)
    local = pl.pallas_call(
        functools.partial(factor_kernel, planes, low_count),
        out_shape=[jax.ShapeDtypeStruct((slots, slots), jnp.bfloat16)] * half,
        in_specs=[vmem] * 2,
        out_specs=[vmem] * half,
        compiler_params=pltpu.CompilerParams(vmem_limit_bytes=8 * 1024 * 1024),
    )(kept, came)
    per_slab = chol_vv.shape[0]
    cut = IRREPS // 2

    def along_x(part):
        return [xor_permute(part, "grp", grp_count, 2 * s) for s in range(1, grp_count // 2)]

    def other_core_of(parts):
        return [xor_permute(part, "grp", grp_count, 1) for part in parts]

    first_half = along_x(chol_vv[:, :cut])

    parts = []
    for (dx, dy), part in zip(planes, local):
        if dx or dy:
            part = plane_permute(part, grp_count, blk_count, dx, dy)
        parts.append(part.astype(jnp.float32))
    total = sum(parts)
    total = after(total, *first_half)
    second_half = along_x(after(chol_vv[:, cut:], total))
    same = [(chol_vv,)] + list(zip(first_half, second_half))
    own_other = other_core_of([chol_vv])
    other = [(own_other[0],)]
    for one, two in zip(first_half, second_half):
        mid = two.shape[1] // 2
        other.append(tuple(other_core_of([one, two[:, :mid], two[:, mid:]])))

    slabs, owners = [], []
    for s in range(grp_count // 2):
        for c, group in enumerate((same, other)):
            for k in range(per_slab):
                slabs.append([part[k] for part in group[s]])
                owners.append((grp ^ (2 * s + c)) * per_slab + k)
    slab_irreps = chol_irrep[jnp.stack(owners)]

    pair_start = (grp * blk_count + blk) * per_dev
    own_pairs = lax.dynamic_slice_in_dim(pair_occ, pair_start, per_dev, 0)
    occ_ids = jnp.arange(occ_irrep.shape[0], dtype=jnp.int32)
    one_hot = own_pairs[:, :, None] == occ_ids[None, None, :]
    labels = jnp.sum(jnp.where(one_hot, occ_irrep[None, None, :], 0), axis=2)
    pair_irrep = jnp.bitwise_xor(labels[:, 0], labels[:, 1])

    scalars = jnp.concatenate([vir_count, pair_irrep, slab_irreps])
    slab_at = IRREPS + per_dev
    split = 2 * per_slab

    bit = low_count
    while bit < blk_count:
        sent = total.astype(jnp.bfloat16)
        if 2 * bit >= blk_count:
            sent, all_rows = lax.optimization_barrier((sent, all_rows))
        came = xor_permute(sent, "blk", blk_count, bit)
        if 2 * bit >= blk_count:
            ladder, masked = ladder_call(
                first_kernel, slab_at, scalars, [all_rows], slabs[:split], per_dev, slots
            )
            came, ladder, masked = lax.optimization_barrier((came, ladder, masked))
        total = total + came.astype(jnp.float32)
        bit *= 2
    scale = 1.0 / math.sqrt(ov_rows * grp_count * blk_count)
    block = (total * scale).astype(jnp.bfloat16)
    got = [
        plane_permute(block, grp_count, blk_count, dx, dy) if dx or dy else block
        for dx, dy in planes
    ]
    if slabs[split:]:
        ladder = ladder_call(
            second_kernel, slab_at + split, scalars, [masked, ladder], slabs[split:], per_dev, slots
        )
    got, ladder = lax.optimization_barrier((tuple(got), ladder))
    same_core = jnp.stack(got)
    other_core = xor_permute(same_core, "grp", grp_count, 1)
    sent = dress_call(scalars, planes, blk_count, ladder, masked, same_core, other_core)
    result = jnp.zeros(amplitudes.shape, jnp.bfloat16)
    result = lax.dynamic_update_slice(result, sent[0], (blk * per_dev, 0, 0, 0))
    top = blk_count // 2
    far, near = list(range(top, blk_count)), list(range(top - 1, 0, -1))
    far = far[1::2] + far[0::2]
    for s in [s for two in zip(far, near + [0]) for s in two if s]:
        came = xor_permute(sent[s], "blk", blk_count, s)
        result = lax.dynamic_update_slice(result, came, ((blk ^ s) * per_dev, 0, 0, 0))
    return result


def solution(mesh):
    return jax.shard_map(
        per_device,
        mesh=mesh,
        in_specs=(
            P("grp", None, "blk", None),
            P("grp", None, None, None),
            P(),
            P(),
            P(),
            P(),
            P(("grp", "blk"), None, None),
            P(("grp", "blk"), None, None),
        ),
        out_specs=P("grp", None, "blk", None),
        check_vma=False,
    )
```
